256 devices in a mesh: dp: 8 (over x, core), expert: 32 (over z, y).
Axes of the slice: x: 4, y: 4, z: 8, core: 2. Of those that a mesh axis runs over, the one named last changes fastest.
Arguments:
- tokens: bfloat16 [32768, 2048], P(('dp', 'expert')), may hold values from -6 to 6
- gates: float32 [32768, 8], P(('dp', 'expert')), may hold values from 0.02 to 0.4
- routes: int32 [32768, 8], P(('dp', 'expert')), may hold values from 0 to 31, all different within a row; in each aligned block of 128 rows (0 to 127, 128 to 255, ...) at most 40 rows name the same one
- cotangent: bfloat16 [32768, 2048], P(('dp', 'expert')), may hold values from -0.29882812 to 0.29882812
- w_in: bfloat16 [32, 2048, 768], P('expert'), may hold values from -0.125 to 0.125
- w_down: bfloat16 [32, 384, 2048], P('expert'), may hold values from -0.3125 to 0.3125
Outputs:
- mixed_out: bfloat16 [32768, 2048], P(('dp', 'expert'))
- grad_gates: float32 [32768, 8], P(('dp', 'expert'))
- grad_in: float32 [32, 2048, 768], P('expert', 'dp')
- grad_down: float32 [32, 384, 2048], P('expert', None, 'dp')
The draws below stay inside these ranges and needn't reach their ends.
Inputs may be any that keep to these rules, and one draw needn't show every extreme that they name: `routes`: among the 128 rows of one device no expert is chosen by more than 40 rows, and on every device some expert is chosen by exactly 40 rows. A row names 8 different experts.
All inputs are finite; a program needn't handle non-finite values.
Results may differ from the reference program's by a relative error of at most 0.0058.
Values may be sent and summed in bfloat16 or wider, within the bound.
No kernel may reach another device: no remote copies, remote signals or barrier semaphores. Data moves between devices by JAX's collectives and lax.ppermute only.
A program may use at most 128 MiB of HBM per device.

```python
import math
import jax
import jax.numpy as jnp
import numpy as np
from jax import lax

D = 2048
FF = 384
TOP = 8
TOK_DEV = 128
EXPERTS = 32
CAP = 40
TOKENS = 32768
N_DP = 8
N_EXPERT = 32


def shard_levels(rng, dims, pieces, low, top_value):
    factor_of, own = 1.0, jax.random.fold_in(rng, 6)
    for dim, blocks in pieces:
        heights = jnp.exp(jax.random.uniform(jax.random.fold_in(own, dim), (blocks,), jnp.float32, low / len(pieces), top_value / len(pieces)))
        factor_of = factor_of * jnp.repeat(heights, dims[dim] // blocks).reshape([-1 if axis == dim else 1 for axis in range(len(dims))])
    return factor_of


def deal_out(key, own, number, rows, number_of, top, bound, skew):
    ranking = jax.random.permutation(key, number_of)
    heavy_load, ordinary = load_shares(number_of, rows * top, bound, skew, True), load_shares(number_of, rows * top, bound, skew, False)
    places = jnp.arange(number_of)

    def named(sizes, rotation):
        used = int((sizes > 0).sum())
        fixed = max(1, used // 4)
        shifted = fixed + (places - fixed + rotation * (used - fixed)) % max(1, number_of - fixed)
        return jnp.zeros((number_of,), jnp.int32).at[ranking[jnp.where(places < fixed, places, shifted)]].set(jnp.asarray(sizes, jnp.int32))

    sizes = jnp.where(number % 4 == 0, named(heavy_load, number // 4), named(ordinary, number - number // 4 - 1))
    mixed = jax.random.permutation(jax.random.fold_in(own, 3), number_of)
    giver, sink = mixed[0:number_of // 2 * 2:2], mixed[1:number_of // 2 * 2:2]
    slack = jnp.minimum(sizes[giver] - 1, bound - sizes[sink]) // 2
    slack = jnp.where((giver == ranking[0]) | (sink == ranking[0]) | (sizes[sink] == 0), 0, jnp.maximum(slack, 0))
    shifted = jax.random.randint(jax.random.fold_in(own, 4), (number_of // 2,), 0, 1 << 20) % (slack + 1)
    sizes = sizes.at[giver].add(-shifted).at[sink].add(shifted)
    labels = jnp.searchsorted(jnp.cumsum(sizes), jnp.arange(rows * top), side="right").astype(jnp.int32)
    listing = labels.reshape(top, rows).T
    listing = listing[jax.random.permutation(jax.random.fold_in(own, 1), rows)]
    rotation = jax.random.randint(jax.random.fold_in(own, 2), (rows, 1), 0, top)
    return jnp.take_along_axis(listing, (jnp.arange(top)[None, :] + rotation) % top, axis=1)


def load_shares(number_of, total, reach, slope, full):
    weights = [(1 << 20) // math.isqrt(standing ** slope) + 1 for standing in range(1, number_of + 1)]
    largest = reach if full else min(reach, max(-(-total // number_of), total * weights[0] // sum(weights)))
    least = 1 if total - largest >= number_of - 1 else 0
    counts, surplus = [largest] + [least] * (number_of - 1), total - largest - least * (number_of - 1)
    while surplus > 0:
        free = [i for i in range(1, number_of) if counts[i] < largest] or [i for i in range(1, number_of) if counts[i] < reach]
        whole, remaining = sum([weights[i] for i in free]), surplus
        for i in free:
            more = min(reach - counts[i], max(1, remaining * weights[i] // whole), surplus)
            counts[i] = counts[i] + more
            surplus = surplus - more
    return np.array(counts)


def centred(own_key, extent, width, most, pieces=(), kind=jnp.bfloat16):
    drawn = width * jax.random.normal(own_key, extent, jnp.float32)
    if pieces:
        drawn = drawn * shard_levels(own_key, extent, pieces, -0.22, 0.18)
    return jnp.clip(drawn, -most, most).astype(kind)


def setup_inputs(seed: int = 0) -> dict:
    streams_of = jax.random.split(jax.random.key(seed), 7)
    tokens = centred(streams_of[0], (TOKENS, D), 1.0, 6.0, ((0, 256),))
    gates = jnp.clip(jnp.exp(math.log(0.4) - 2.9957323 * jax.random.uniform(streams_of[1], (TOKENS, TOP), jnp.float32) ** shard_levels(streams_of[1], (TOKENS, TOP), ((0, 256),), -0.2, 0.2)), 0.02, 0.4)
    routes_keys = jax.random.split(jax.random.fold_in(streams_of[2], 1), TOKENS // TOK_DEV)
    routes_turns = jax.random.permutation(jax.random.fold_in(streams_of[2], 3), TOKENS // TOK_DEV)
    routes = jax.vmap(lambda own, number: deal_out(jax.random.fold_in(streams_of[2], 2), own, number, TOK_DEV, EXPERTS, TOP, CAP, 1))(routes_keys, routes_turns).reshape((TOKENS, TOP))
    cotangent = centred(streams_of[3], (TOKENS, D), 0.05, 0.29882812, ((0, 256),))
    w_in = centred(streams_of[4], (EXPERTS, D, 2 * FF), D ** -0.5, 0.125, ((0, 32),))
    w_down = centred(streams_of[5], (EXPERTS, FF, D), FF ** -0.5, 0.3125, ((0, 32),))
    return dict(tokens=tokens, gates=gates, routes=routes, cotangent=cotangent, w_in=w_in, w_down=w_down)


def swiglu_rows(rows_in, w_in_e, w_down_e):
    hidden = w_down_e.shape[0]
    projected = jnp.dot(rows_in, w_in_e, preferred_element_type=jnp.float32)
    gate_pre = projected[:, :hidden]
    up_pre = projected[:, hidden:]
    sig_gate = jax.nn.sigmoid(gate_pre)
    hidden_act = (gate_pre * sig_gate * up_pre).astype(jnp.bfloat16)
    expert_out = jnp.dot(hidden_act, w_down_e, preferred_element_type=jnp.float32).astype(jnp.bfloat16)
    return gate_pre, up_pre, sig_gate, hidden_act, expert_out


def backward_rows(rows_in, gate_pre, up_pre, sig_gate, hidden_act, scaled_cot, w_down_e):
    grad_down_part = lax.dot_general(hidden_act, scaled_cot, (((0,), (0,)), ((), ())), preferred_element_type=jnp.float32)
    grad_hidden = lax.dot_general(scaled_cot, w_down_e, (((1,), (1,)), ((), ())), preferred_element_type=jnp.float32)
    grad_up_pre = grad_hidden * gate_pre * sig_gate
    grad_gate_pre = grad_hidden * up_pre * sig_gate * (1.0 + gate_pre * (1.0 - sig_gate))
    grad_pre = jnp.concatenate([grad_gate_pre, grad_up_pre], 1).astype(jnp.bfloat16)
    grad_in_part = lax.dot_general(rows_in, grad_pre, (((0,), (0,)), ((), ())), preferred_element_type=jnp.float32)
    return grad_in_part, grad_down_part


def reference(tokens, gates, routes, cotangent, w_in, w_down):
    model_width = tokens.shape[1]
    flat_routes = routes.reshape(-1)
    gate_flat = gates.reshape(-1)
    cot_float = cotangent.astype(jnp.float32)
    row_bound = N_DP * N_EXPERT * CAP

    def per_expert(state_pair, expert):
        mixed_acc, grad_gate_acc = state_pair
        is_hit = flat_routes == expert
        row_index = jnp.nonzero(is_hit, size=row_bound, fill_value=0)[0].astype(jnp.int32)
        is_valid = jnp.arange(row_bound, dtype=jnp.int32) < jnp.sum(is_hit.astype(jnp.int32))
        token_index = row_index // TOP
        rows_in = jnp.where(is_valid[:, None], tokens[token_index], jnp.zeros((), tokens.dtype))
        w_down_e = w_down[expert]
        gate_pre, up_pre, sig_gate, hidden_act, expert_out = swiglu_rows(rows_in, w_in[expert], w_down_e)
        out_float = expert_out.astype(jnp.float32)
        weight_rows = jnp.where(is_valid, gate_flat[row_index], jnp.zeros((), jnp.float32))
        mixed_acc = mixed_acc.at[token_index].add(weight_rows[:, None] * out_float)
        inner = jnp.sum(cot_float[token_index] * out_float, 1)
        grad_gate_acc = grad_gate_acc.at[row_index].add(jnp.where(is_valid, inner, jnp.zeros((), jnp.float32)))
        scaled_cot = (weight_rows[:, None] * cot_float[token_index]).astype(jnp.bfloat16)
        grad_in_part, grad_down_part = backward_rows(rows_in, gate_pre, up_pre, sig_gate, hidden_act, scaled_cot, w_down_e)
        return (mixed_acc, grad_gate_acc), (grad_in_part, grad_down_part)

    start_state = (jnp.zeros((TOKENS, model_width), jnp.float32), jnp.zeros((TOKENS * TOP,), jnp.float32))
    final_state, grads = lax.scan(per_expert, start_state, jnp.arange(EXPERTS, dtype=jnp.int32))
    mixed_acc, grad_gate_acc = final_state
    grad_in, grad_down = grads
    return mixed_acc.astype(jnp.bfloat16), grad_gate_acc.reshape(TOKENS, TOP), grad_in, grad_down
```

```python
import jax
import jax.numpy as jnp
from jax import lax
from jax.experimental import pallas as pl
from jax.experimental.pallas import tpu as pltpu
from jax.sharding import Mesh, PartitionSpec as P

BF16 = jnp.bfloat16
F32 = jnp.float32
VMEM_BYTES = 60 * 1024 * 1024
TILE = 256


def params(steps=1):
    return pltpu.CompilerParams(
        dimension_semantics=("arbitrary",) * steps, vmem_limit_bytes=VMEM_BYTES
    )


def cost(flops, moved):
    return pl.CostEstimate(flops=flops, bytes_accessed=moved, transcendentals=0)


def forward_kernel(x_ref, w_ref, silu_ref, slope_ref, hidden_ref):
    rows, width = x_ref.shape
    hidden = hidden_ref.shape[2]
    w = w_ref[...].reshape(width, 2 * hidden)

    @pl.loop(0, rows // TILE)
    def _(i):
        part = pl.ds(pl.multiple_of(i * TILE, TILE), TILE)
        pre = jnp.dot(x_ref[part, :], w, preferred_element_type=F32)
        gate_pre, up_pre = pre[:, :hidden], pre[:, hidden:]
        sig = jax.nn.sigmoid(gate_pre)
        silu = gate_pre * sig
        silu_ref[0, part, :] = silu.astype(BF16)
        slope_ref[0, part, :] = (up_pre * sig * (1.0 + gate_pre * (1.0 - sig))).astype(BF16)
        hidden_ref[0, part, :] = (silu * up_pre).astype(BF16)


def forward(x, w_in_all):
    rows, width = x.shape
    shares, experts, depth, columns = w_in_all.shape
    hidden = columns // 2
    out = jax.ShapeDtypeStruct((experts, rows, hidden), BF16)
    spec = pl.BlockSpec((1, rows, hidden), lambda e: (e, 0, 0))
    return pl.pallas_call(
        forward_kernel,
        grid=(experts,),
        in_specs=[
            pl.BlockSpec((rows, width), lambda e: (0, 0)),
            pl.BlockSpec((shares, 1, depth, columns), lambda e: (0, e, 0, 0)),
        ],
        out_specs=[spec] * 3,
        out_shape=[out] * 3,
        compiler_params=params(),
        cost_estimate=cost(2 * rows * width * columns * experts, 26 << 20),
    )(x, w_in_all)


def hidden_kernel(c_ref, w_ref, g_ref, silu_ref, slope_ref, hidden_ref, pre_ref, hs_ref, hst_ref, gg_ref):
    expert = pl.program_id(0)
    rows, width = c_ref.shape
    hidden = hidden_ref.shape[2]
    w = w_ref[...].reshape(hidden, width)

    @pl.when(expert == 0)
    def _():
        gg_ref[...] = jnp.zeros_like(gg_ref)

    @pl.loop(0, rows // TILE)
    def _(i):
        part = pl.ds(pl.multiple_of(i * TILE, TILE), TILE)
        raw = lax.dot_general(
            c_ref[part, :], w, (((1,), (1,)), ((), ())), preferred_element_type=F32
        )
        lane = lax.broadcasted_iota(jnp.int32, (TILE, g_ref.shape[1]), 1)
        gate = jnp.sum(jnp.where(lane == expert, g_ref[part, :], 0.0), 1, keepdims=True)
        act = hidden_ref[0, part, :].astype(F32)
        inner = jnp.sum(act * raw, 1, keepdims=True)
        gg_ref[part, :] += jnp.where(lane == expert, inner, 0.0)
        scaled = (act * gate).astype(BF16)
        hs_ref[0, part, :] = scaled
        hst_ref[0, :, part] = scaled.T
        grad = raw * gate
        pre_ref[0, part, :hidden] = (grad * slope_ref[0, part, :].astype(F32)).astype(BF16)
        pre_ref[0, part, hidden:] = (grad * silu_ref[0, part, :].astype(F32)).astype(BF16)


def hidden_gradient(c, w_down_all, gates, silu, slope, act):
    rows, width = c.shape
    shares, experts, depth, _ = w_down_all.shape
    hidden = shares * depth
    spec = pl.BlockSpec((1, rows, hidden), lambda e: (e, 0, 0))
    small = pl.BlockSpec((rows, experts), lambda e: (0, 0))
    return pl.pallas_call(
        hidden_kernel,
        grid=(experts,),
        in_specs=[
            pl.BlockSpec((rows, width), lambda e: (0, 0)),
            pl.BlockSpec((shares, 1, depth, width), lambda e: (0, e, 0, 0)),
            small,
            spec,
            spec,
            spec,
        ],
        out_specs=[
            pl.BlockSpec((1, rows, 2 * hidden), lambda e: (e, 0, 0)),
            spec,
            pl.BlockSpec((1, hidden, rows), lambda e: (e, 0, 0)),
            small,
        ],
        out_shape=[
            jax.ShapeDtypeStruct((experts, rows, 2 * hidden), BF16),
            jax.ShapeDtypeStruct((experts, rows, hidden), BF16),
            jax.ShapeDtypeStruct((experts, hidden, rows), BF16),
            jax.ShapeDtypeStruct((rows, experts), F32),
        ],
        compiler_params=params(),
        cost_estimate=cost(2 * rows * width * hidden * experts, 32 << 20),
    )(c, w_down_all, gates, silu, slope, act)


def output_kernel(place_ref, hs_ref, w_ref, out_ref):
    experts, rows, hidden = hs_ref.shape
    width = w_ref.shape[3]
    blocks, block, _ = out_ref.shape
    per_tile = TILE // block

    @pl.loop(0, rows // TILE)
    def _(i):
        part = pl.ds(pl.multiple_of(i * TILE, TILE), TILE)
        total = jnp.zeros((TILE, width), F32)
        for e in range(experts):
            total += jnp.dot(
                hs_ref[e, part, :], w_ref[:, e].reshape(hidden, width), preferred_element_type=F32
            )
        for j in range(per_tile):
            out_ref[pl.ds(place_ref[i * per_tile + j], 1)] = (
                total[j * block : (j + 1) * block].astype(BF16).reshape(1, block, width)
            )


def output_rows(place, hs, w_down_all, block):
    experts, rows, hidden = hs.shape
    shares, _, depth, width = w_down_all.shape
    blocks = rows // block
    columns = 512
    return pl.pallas_call(
        output_kernel,
        grid_spec=pltpu.PrefetchScalarGridSpec(
            num_scalar_prefetch=1,
            grid=(width // columns,),
            in_specs=[
                pl.BlockSpec((experts, rows, hidden), lambda n, p: (0, 0, 0)),
                pl.BlockSpec((shares, experts, depth, columns), lambda n, p: (0, 0, 0, n)),
            ],
            out_specs=pl.BlockSpec((blocks, block, columns), lambda n, p: (0, 0, n)),
        ),
        out_shape=jax.ShapeDtypeStruct((blocks, block, width), BF16),
        compiler_params=params(),
        cost_estimate=cost(2 * rows * width * hidden * experts, 14 << 20),
    )(place, hs, w_down_all)


def weight_kernel(place_ref, x_ref, c_ref, pre_ref, hst_ref, first_ref, second_ref):
    experts, rows, columns = pre_ref.shape
    hidden = hst_ref.shape[1]
    share = x_ref.shape[1]
    half = first_ref.shape[2]
    xt = x_ref[...].T
    c = c_ref[...]

    @pl.loop(0, experts)
    def _(j):
        e = place_ref[j]
        grad_in = jnp.dot(xt, pre_ref[e], preferred_element_type=F32).astype(BF16)
        grad_down = jnp.dot(hst_ref[e], c, preferred_element_type=F32).astype(BF16)
        first_ref[pl.ds(j, 1), 0] = grad_in[:half].reshape(1, half, columns)
        second_ref[0, pl.ds(j, 1), : share - half] = grad_in[half:].reshape(1, share - half, columns)
        piece = hidden // 3
        for i in range(3):
            second_ref[0, pl.ds(j, 1), share - half :, i * share : (i + 1) * share] = grad_down[
                i * piece : (i + 1) * piece
            ].reshape(1, piece, share)


def weight_gradient(place, x, c, pre, hst, ring):
    experts, rows, columns = pre.shape
    hidden = hst.shape[1]
    share = x.shape[1] // (2 * ring)
    half = (share + hidden // 3) // 2
    first = jax.ShapeDtypeStruct((experts, ring, half, columns), BF16)
    second = jax.ShapeDtypeStruct((ring, experts, half, columns), BF16)
    return pl.pallas_call(
        weight_kernel,
        grid_spec=pltpu.PrefetchScalarGridSpec(
            num_scalar_prefetch=1,
            grid=(ring,),
            in_specs=[
                pl.BlockSpec((rows, share), lambda s, p: (0, p[4 + s])),
                pl.BlockSpec((rows, share), lambda s, p: (0, p[4 + s])),
                pl.BlockSpec((experts, rows, columns), lambda s, p: (0, 0, 0)),
                pl.BlockSpec((experts, hidden, rows), lambda s, p: (0, 0, 0)),
            ],
            out_specs=[
                pl.BlockSpec((experts, 1, half, columns), lambda s, p: (0, s, 0, 0)),
                pl.BlockSpec((1, experts, half, columns), lambda s, p: (s, 0, 0, 0)),
            ],
        ),
        out_shape=[first, second],
        compiler_params=params(),
        cost_estimate=cost(rows * x.shape[1] * 3 * hidden * experts, 27 << 20),
    )(place, x, c, pre, hst)


def up(n):
    return [(i, (i + 1) % n) for i in range(n)]


def down(n):
    return [((i + 1) % n, i) for i in range(n)]


def ring_gather(block, axis):
    n = lax.axis_size(axis)
    half = block.shape[0] // 2
    got = {0: block}
    above = below = block
    for step in range(1, n // 2):
        below = lax.ppermute(below, axis, up(n))
        above = lax.ppermute(above, axis, down(n))
        got[step], got[n - step] = below, above
    got[n // 2] = jnp.concatenate(
        [lax.ppermute(below[:half], axis, up(n)), lax.ppermute(above[half:], axis, down(n))], 0
    )
    return jnp.concatenate([got[i] for i in range(n)], 0)


def add(*terms):
    total = terms[0].astype(F32)
    for term in terms[1:]:
        total = total + term.astype(F32)
    return total


def ring_scatter(parts, axis, kind):
    half = parts[0].shape[0] // 2
    low = lax.ppermute(parts[2][:half], axis, up(4))
    high = lax.ppermute(parts[2][half:], axis, down(4))
    to_up = jnp.concatenate([add(parts[1][:half], low).astype(BF16), parts[1][half:]], 0)
    to_down = jnp.concatenate([parts[3][:half], add(parts[3][half:], high).astype(BF16)], 0)
    low = lax.ppermute(to_up, axis, up(4))
    high = lax.ppermute(to_down, axis, down(4))
    return add(parts[0], low, high).astype(kind)


def on_device(tokens, gates, routes, cotangent, w_in, w_down):
    block, width = tokens.shape
    hidden = w_down.shape[1]
    x_at, core_at = lax.axis_index("x"), lax.axis_index("core")
    z_at, y_at = lax.axis_index("z"), lax.axis_index("y")
    z_size, y_size = lax.axis_size("z"), lax.axis_size("y")
    share_at = x_at * 2 + core_at

    small = jnp.concatenate([routes.T.astype(F32), gates.T], 0)
    small = lax.all_gather(small, "z", axis=0)
    order = jnp.remainder(z_at - jnp.arange(z_size), z_size)
    small = small[order]
    top = routes.shape[1]
    ring_routes, ring_gates = small[:, :top].astype(jnp.int32), small[:, top:]
    mine = z_at * y_size + jnp.arange(y_size)
    hit = ring_routes[:, None] == mine[None, :, None, None]
    gate_of = jnp.sum(jnp.where(hit, ring_gates[:, None], 0.0), 2)
    gate_of = jnp.swapaxes(gate_of, 1, 2).reshape(z_size * block, y_size)

    depth_in, depth_down = width // 8, hidden // 8
    share_in = lax.dynamic_slice_in_dim(w_in[0], share_at * depth_in, depth_in, 0)
    share_down = lax.dynamic_slice_in_dim(w_down[0], share_at * depth_down, depth_down, 0)
    w_in_all = lax.all_gather(share_in, ("x", "core", "y"), axis=0, tiled=True)
    w_in_all = w_in_all.reshape(8, y_size, depth_in, 2 * hidden)
    w_down_all = lax.all_gather(share_down, ("x", "core", "y"), axis=0, tiled=True)
    w_down_all = w_down_all.reshape(8, y_size, depth_down, width)

    ring_tokens = ring_gather(tokens, "z")
    ring_cot = ring_gather(cotangent, "z")

    silu, slope, act = forward(ring_tokens, w_in_all)
    pre, hs, hst, gg = hidden_gradient(ring_cot, w_down_all, gate_of, silu, slope, act)

    experts_at = jnp.remainder(y_at + jnp.arange(4), 4)
    shares_at = jnp.remainder(x_at + jnp.arange(4), 4) * 2

    def grads(core):
        place = jnp.concatenate([experts_at, shares_at + core]).astype(jnp.int32)
        return weight_gradient(place, ring_tokens, ring_cot, pre, hst, 4)

    other = grads(1 - core_at)
    swap = [(0, 1), (1, 0)]
    other = [lax.ppermute(g, "core", swap) for g in other]
    partial = output_rows(order.astype(jnp.int32), hs, w_down_all, block)
    mixed_out = lax.psum_scatter(partial, "z", scatter_dimension=0, tiled=True)[0]
    own = grads(core_at)
    first, second = [add(g, h).astype(BF16) for g, h in zip(own, other)]
    first = ring_scatter([first[i] for i in range(4)], "y", BF16)
    second = ring_scatter([second[i] for i in range(4)], "x", BF16)
    first = ring_scatter([first[i] for i in range(4)], "x", F32)
    second = ring_scatter([second[i] for i in range(4)], "y", F32)

    rest = depth_in - first.shape[0]
    grad_in = jnp.concatenate([first, second[:rest]], 0)
    packed = second[rest:]
    grad_down = jnp.concatenate(
        [packed[:, i * depth_in : (i + 1) * depth_in] for i in range(3)], 0
    )

    gg = jnp.swapaxes(gg.reshape(z_size, block, y_size), 1, 2)
    gg = jnp.sum(jnp.where(hit, gg[:, :, None], 0.0), 1)
    grad_gates = lax.psum_scatter(gg[order], "z", scatter_dimension=0, tiled=True)[0].T
    return mixed_out, grad_gates, grad_in[None], grad_down[None]


def solution(mesh):
    wide = Mesh(mesh.devices.reshape(4, 2, 8, 4), ("x", "core", "z", "y"))
    rows = P(("x", "core", "z", "y"), None)
    expert = P(("z", "y"), None, None)
    return jax.shard_map(
        on_device,
        mesh=wide,
        in_specs=(rows, rows, rows, rows, expert, expert),
        out_specs=(
            rows,
            rows,
            P(("z", "y"), ("x", "core"), None),
            P(("z", "y"), None, ("x", "core")),
        ),
        check_vma=False,
    )
```

```python
import jax
import jax.numpy as jnp
from jax import lax
from jax.experimental import pallas as pl
from jax.experimental.pallas import tpu as pltpu
from jax.sharding import Mesh, PartitionSpec as P

BF16 = jnp.bfloat16
F32 = jnp.float32
VMEM_BYTES = 48 * 1024 * 1024
SLOTS = 80
PAIRS = ((1, 7), (2, 6), (3, 5), (0, 4))
DISTANCES = tuple(d for pair in PAIRS for d in pair)


def params(steps=1):
    return pltpu.CompilerParams(
        dimension_semantics=("arbitrary",) * steps, vmem_limit_bytes=VMEM_BYTES
    )


def cost(flops, moved):
    return pl.CostEstimate(flops=flops, bytes_accessed=moved, transcendentals=0)


def chosen(slot_row):
    tokens = slot_row.shape[1]
    return lax.broadcasted_iota(jnp.int32, (SLOTS, tokens), 0) == slot_row


def select_kernel(count, *refs):
    slot_ref, pieces, out_ref, rows_ref = refs[0], refs[1 : 1 + count], refs[-2], refs[-1]
    experts = slot_ref.shape[1]
    at = 0
    for piece in pieces:
        rows_ref[at : at + piece.shape[0], :] = piece[...]
        at += piece.shape[0]
    pick = jnp.concatenate(
        [chosen(slot_ref[0, e : e + 1, :]).astype(BF16) for e in range(experts)], 0
    )
    width = rows_ref.shape[1]
    for n in range(0, width, 512):
        got = jnp.dot(pick, rows_ref[:, n : n + 512], preferred_element_type=F32).astype(BF16)
        out_ref[:, 0, :, n : n + 512] = got.reshape(experts, SLOTS, 512)


def select(pair, slots, pieces, buffer):
    pairs, experts, tokens = slots.shape
    width = pieces[0].shape[1]
    operands = [slots, *pieces]
    in_specs = [pl.BlockSpec((1, experts, tokens), lambda i: (pair, 0, 0))]
    in_specs += [pl.BlockSpec(piece.shape, lambda i: (0, 0)) for piece in pieces]
    aliases = {}
    if buffer is not None:
        aliases = {len(operands): 0}
        operands.append(buffer)
        in_specs.append(pl.BlockSpec(memory_space=pl.ANY))
    count = len(pieces)
    return pl.pallas_call(
        lambda *refs: select_kernel(count, *refs),
        grid=(1,),
        in_specs=in_specs,
        out_specs=pl.BlockSpec((experts, 1, SLOTS, width), lambda i: (0, pair, 0, 0)),
        out_shape=jax.ShapeDtypeStruct((experts, pairs, SLOTS, width), BF16),
        scratch_shapes=[pltpu.VMEM((tokens, width), BF16)],
        input_output_aliases=aliases,
        compiler_params=params(),
        cost_estimate=cost(2 * experts * SLOTS * tokens * width, 3 << 20),
    )(*operands)


def forward_kernel(place_ref, x_ref, w_ref, silu_ref, slope_ref, hidden_ref):
    width = x_ref.shape[2]
    hidden = hidden_ref.shape[2]
    w = w_ref[...].reshape(width, 2 * hidden)
    pre = jnp.dot(x_ref[0], w, preferred_element_type=F32)
    gate_pre, up_pre = pre[:, :hidden], pre[:, hidden:]
    sig = jax.nn.sigmoid(gate_pre)
    silu = gate_pre * sig
    silu_ref[0] = silu.astype(BF16)
    slope_ref[0] = (up_pre * sig * (1.0 + gate_pre * (1.0 - sig))).astype(BF16)
    hidden_ref[0] = (silu * up_pre).astype(BF16)


def forward(place, x, w_in_all):
    experts, rows, width = x.shape
    shares, _, depth, columns = w_in_all.shape
    hidden = columns // 2
    out = jax.ShapeDtypeStruct((experts, rows, hidden), BF16)
    spec = pl.BlockSpec((1, rows, hidden), lambda e, p: (e, 0, 0))
    return pl.pallas_call(
        forward_kernel,
        grid_spec=pltpu.PrefetchScalarGridSpec(
            num_scalar_prefetch=1,
            grid=(experts,),
            in_specs=[
                pl.BlockSpec((1, rows, width), lambda e, p: (e, 0, 0)),
                pl.BlockSpec((shares, 1, depth, columns), lambda e, p: (0, p[e], 0, 0)),
            ],
            out_specs=[spec] * 3,
        ),
        out_shape=[out] * 3,
        compiler_params=params(),
        cost_estimate=cost(2 * rows * width * columns * experts, 21 << 20),
    )(place, x, w_in_all)


def hidden_kernel(
    core_ref, c_ref, w_ref, slot_ref, gate_ref, silu_ref, slope_ref, hidden_ref,
    pre_ref, hst_ref, y_ref, gg_ref,
):
    rows, width = c_ref.shape[1:]
    hidden = hidden_ref.shape[2]
    half = width // 2
    pairs = slot_ref.shape[1]
    own = pl.ds(pl.multiple_of(core_ref[0] * half, half), half)
    other = pl.ds(pl.multiple_of((1 - core_ref[0]) * half, half), half)
    across = (((1,), (1,)), ((), ()))
    raw = lax.dot_general(c_ref[0, :, own], w_ref[0, 0], across, preferred_element_type=F32)
    raw += lax.dot_general(c_ref[0, :, other], w_ref[0, 1], across, preferred_element_type=F32)
    picks = [chosen(slot_ref[0, p : p + 1, :]) for p in range(pairs)]
    gate = jnp.concatenate(
        [
            jnp.sum(jnp.where(picks[p], gate_ref[0, p : p + 1, :], 0.0), 1, keepdims=True)
            for p in range(pairs)
        ],
        0,
    )
    act = hidden_ref[0]
    for part, at in ((0, own), (1, other)):
        out = jnp.dot(act, w_ref[0, part], preferred_element_type=F32)
        y_ref[0, :, at] = (out * gate).astype(BF16)
    act = act.astype(F32)
    inner = jnp.sum(act * raw, 1, keepdims=True)
    for p in range(pairs):
        gg_ref[0, p : p + 1, :] = jnp.sum(
            jnp.where(picks[p], inner[p * SLOTS : (p + 1) * SLOTS], 0.0), 0, keepdims=True
        )
    hst_ref[0] = (act * gate).astype(BF16).T
    grad = raw * gate
    pre_ref[0, :, :hidden] = (grad * slope_ref[0].astype(F32)).astype(BF16)
    pre_ref[0, :, hidden:] = (grad * silu_ref[0].astype(F32)).astype(BF16)


def hidden_gradient(core, c, w_down_all, slots, gates, silu, slope, act):
    experts, rows, width = c.shape
    hidden = w_down_all.shape[2]
    _, pairs, tokens = slots.shape
    one = lambda *shape: pl.BlockSpec((1, *shape), lambda e, p: (e,) + (0,) * len(shape))
    wide = one(rows, hidden)
    return pl.pallas_call(
        hidden_kernel,
        grid_spec=pltpu.PrefetchScalarGridSpec(
            num_scalar_prefetch=1,
            grid=(experts,),
            in_specs=[
                one(rows, width),
                one(2, hidden, width // 2),
                one(pairs, tokens),
                one(pairs, tokens),
                wide,
                wide,
                wide,
            ],
            out_specs=[
                one(rows, 2 * hidden),
                one(hidden, rows),
                one(rows, width),
                one(pairs, tokens),
            ],
        ),
        out_shape=[
            jax.ShapeDtypeStruct((experts, rows, 2 * hidden), BF16),
            jax.ShapeDtypeStruct((experts, hidden, rows), BF16),
            jax.ShapeDtypeStruct((experts, rows, width), BF16),
            jax.ShapeDtypeStruct((experts, pairs, tokens), F32),
        ],
        compiler_params=params(),
        cost_estimate=cost(4 * rows * width * hidden * experts, 23 << 20),
    )(core, c, w_down_all, slots, gates, silu, slope, act)


def output_kernel(place_ref, slot_ref, y_ref, out_ref, pick_ref):
    pairs, experts, tokens = slot_ref.shape
    block = tokens // 2
    columns = out_ref.shape[2]

    @pl.when(pl.program_id(0) == 0)
    def _():
        for p in range(pairs):
            pick = jnp.concatenate(
                [chosen(slot_ref[p, e : e + 1, :]).astype(BF16) for e in range(experts)], 0
            )
            pick_ref[p] = pick.T

    for p in range(pairs):
        y = y_ref[:, p].reshape(experts * SLOTS, columns)
        total = jnp.dot(pick_ref[p], y, preferred_element_type=F32).astype(BF16)
        for j in range(2):
            out_ref[pl.ds(place_ref[2 * p + j], 1)] = total[j * block : (j + 1) * block].reshape(
                1, block, columns
            )


def output_rows(place, slots, y):
    pairs, experts, tokens = slots.shape
    width = y.shape[3]
    columns = 512
    return pl.pallas_call(
        output_kernel,
        grid_spec=pltpu.PrefetchScalarGridSpec(
            num_scalar_prefetch=1,
            grid=(width // columns,),
            in_specs=[
                pl.BlockSpec((pairs, experts, tokens), lambda n, p: (0, 0, 0)),
                pl.BlockSpec((experts, pairs, SLOTS, columns), lambda n, p: (0, 0, 0, n)),
            ],
            out_specs=pl.BlockSpec((2 * pairs, tokens // 2, columns), lambda n, p: (0, 0, n)),
            scratch_shapes=[pltpu.VMEM((pairs, tokens, experts * SLOTS), BF16)],
        ),
        out_shape=jax.ShapeDtypeStruct((2 * pairs, tokens // 2, width), BF16),
        compiler_params=params(),
        cost_estimate=cost(2 * pairs * experts * SLOTS * tokens * width, 10 << 20),
    )(place, slots, y)


def weight_kernel(more, place_ref, x_ref, c_ref, pre_ref, hst_ref, *refs):
    first_ref, second_ref = refs[-2:]
    experts, rows, columns = pre_ref.shape
    hidden = hst_ref.shape[1]
    share = x_ref.shape[2]
    half = first_ref.shape[2]
    rest, piece = share - half, hidden // 3
    for e in range(experts):
        grad_in = jnp.dot(x_ref[e].T, pre_ref[e], preferred_element_type=F32)
        grad_down = jnp.dot(hst_ref[e], c_ref[e], preferred_element_type=F32)
        packed = jnp.concatenate(
            [grad_down[i * piece : (i + 1) * piece] for i in range(3)], 1
        )
        first, second = grad_in[:half], jnp.concatenate([grad_in[half:], packed], 0)
        if more:
            first += refs[0][e, 0].astype(F32)
            second += refs[1][0, e].astype(F32)
        first_ref[e, 0] = first.astype(BF16)
        second_ref[0, e] = second.astype(BF16)


def weight_gradient(place, x, c, pre, hst, ring, other):
    experts, rows, columns = pre.shape
    hidden = hst.shape[1]
    share = x.shape[2] // (2 * ring)
    half = (share + hidden // 3) // 2
    parts = [
        pl.BlockSpec((experts, 1, half, columns), lambda s, p: (0, s, 0, 0)),
        pl.BlockSpec((1, experts, half, columns), lambda s, p: (s, 0, 0, 0)),
    ]
    more = bool(other)
    return pl.pallas_call(
        lambda *refs: weight_kernel(more, *refs),
        grid_spec=pltpu.PrefetchScalarGridSpec(
            num_scalar_prefetch=1,
            grid=(ring,),
            in_specs=[
                pl.BlockSpec((experts, rows, share), lambda s, p: (0, 0, p[s])),
                pl.BlockSpec((experts, rows, share), lambda s, p: (0, 0, p[s])),
                pl.BlockSpec((experts, rows, columns), lambda s, p: (0, 0, 0)),
                pl.BlockSpec((experts, hidden, rows), lambda s, p: (0, 0, 0)),
            ]
            + parts * more,
            out_specs=parts,
        ),
        out_shape=[
            jax.ShapeDtypeStruct((experts, ring, half, columns), BF16),
            jax.ShapeDtypeStruct((ring, experts, half, columns), BF16),
        ],
        compiler_params=params(),
        cost_estimate=cost(rows * x.shape[2] * 3 * hidden * experts, 20 << 20),
    )(place, x, c, pre, hst, *other)


def shift(value, axis, by):
    n = lax.axis_size(axis)
    return lax.ppermute(value, axis, [(i, (i + by) % n) for i in range(n)])


def ring_blocks(block, axis):
    n = lax.axis_size(axis)
    half = block.shape[0] // 2
    got = {0: [block]}
    below = above = block
    for step in range(1, n // 2):
        below, above = shift(below, axis, 1), shift(above, axis, -1)
        got[step], got[n - step] = [below], [above]
    got[n // 2] = [shift(below[:half], axis, 1), shift(above[half:], axis, -1)]
    return got


def add(*terms):
    total = terms[0].astype(F32)
    for term in terms[1:]:
        total = total + term.astype(F32)
    return total


def ring_scatter(parts, axis, kind):
    half = parts[0].shape[0] // 2
    low = shift(parts[2][:half], axis, 1)
    high = shift(parts[2][half:], axis, -1)
    to_up = jnp.concatenate([add(parts[1][:half], low).astype(BF16), parts[1][half:]], 0)
    to_down = jnp.concatenate([parts[3][:half], add(parts[3][half:], high).astype(BF16)], 0)
    low, high = shift(to_up, axis, 1), shift(to_down, axis, -1)
    return add(parts[0], low, high).astype(kind)


def swap_cores(value):
    return lax.ppermute(value, "core", [(0, 1), (1, 0)])


def on_device(tokens, gates, routes, cotangent, w_in, w_down):
    block, width = tokens.shape
    hidden = w_down.shape[1]
    top = routes.shape[1]
    x_at, core_at = lax.axis_index("x"), lax.axis_index("core")
    z_at, y_at = lax.axis_index("z"), lax.axis_index("y")
    z_size, y_size = lax.axis_size("z"), lax.axis_size("y")
    pairs = len(PAIRS)
    experts_at = jnp.remainder(y_at + jnp.arange(y_size), y_size).astype(jnp.int32)

    depth = width // 8
    share_in = lax.dynamic_slice_in_dim(w_in[0], (x_at * 2 + core_at) * depth, depth, 0)
    w_in_all = lax.all_gather(share_in, ("x", "core", "y"), axis=0, tiled=True)
    w_in_all = w_in_all.reshape(8, y_size, depth, 2 * hidden)

    small = jnp.concatenate([routes.T.astype(F32), gates.T], 0)[None]
    order = [0]
    for by in (4, 2, 1):
        small = jnp.concatenate([small, shift(small, "z", by)], 0)
        order += [o + by for o in order]
    small = jnp.stack([small[order.index(d)] for d in DISTANCES])
    ring_routes, ring_gates = small[:, :top].astype(jnp.int32), small[:, top:]
    hit = ring_routes[:, None] == (z_at * y_size + experts_at)[None, :, None, None]
    gate_of = jnp.sum(jnp.where(hit, ring_gates[:, None], 0.0), 2)
    any_hit = jnp.any(hit, 2)
    earlier = jnp.arange(block)[:, None] < jnp.arange(block)[None, :]
    slot = jnp.dot(
        any_hit.reshape(-1, block).astype(BF16), earlier.astype(BF16), preferred_element_type=F32
    )
    slot = slot.reshape(pairs, 2, y_size, block).astype(jnp.int32)
    slot = slot + (SLOTS // 2) * jnp.arange(2, dtype=jnp.int32)[None, :, None, None]
    slot = jnp.where(any_hit.reshape(slot.shape), slot, -1)
    slots = jnp.swapaxes(slot, 1, 2).reshape(pairs, y_size, 2 * block)
    expert_slots = jnp.swapaxes(slots, 0, 1)
    gate_of = gate_of.reshape(pairs, 2, y_size, block).transpose(2, 0, 1, 3)
    gate_of = gate_of.reshape(y_size, pairs, 2 * block)

    half = width // 2
    own = lax.dynamic_slice_in_dim(w_down[0], core_at * half, half, 1)
    rest = lax.dynamic_slice_in_dim(w_down[0], (1 - core_at) * half, half, 1)
    below, above = shift(own, "y", 1), shift(own, "y", -1)
    cut = hidden // 2
    far = jnp.concatenate([shift(below[:cut], "y", 1), shift(above[cut:], "y", -1)], 0)
    w_down_all = jnp.stack(
        [jnp.stack([own, rest])]
        + [jnp.stack([held, swap_cores(held)]) for held in (above, far, below)]
    )

    def routed(rows):
        got = ring_blocks(rows, "z")
        buffer = None
        for p, (a, b) in enumerate(PAIRS):
            buffer = select(p, slots, got[a] + got[b], buffer)
        return buffer.reshape(y_size, pairs * SLOTS, width)

    rows_in = routed(tokens)
    rows_cot = routed(cotangent)
    silu, slope, act = forward(experts_at, rows_in, w_in_all)
    pre, hst, y, gg = hidden_gradient(
        core_at.astype(jnp.int32)[None], rows_cot, w_down_all, expert_slots, gate_of,
        silu, slope, act,
    )

    shares_at = jnp.remainder(x_at + jnp.arange(4), 4).astype(jnp.int32) * 2
    other = weight_gradient(shares_at + 1 - core_at, rows_in, rows_cot, pre, hst, 4, [])
    other = [swap_cores(g) for g in other]
    place = jnp.remainder(z_at - jnp.array(DISTANCES), z_size).astype(jnp.int32)
    partial = output_rows(place, slots, y.reshape(y_size, pairs, SLOTS, width))
    mixed_out = lax.psum_scatter(partial, "z", scatter_dimension=0, tiled=True)[0]
    first, second = weight_gradient(
        shares_at + core_at, rows_in, rows_cot, pre, hst, 4, other
    )
    first = ring_scatter([first[i] for i in range(4)], "y", BF16)
    second = ring_scatter([second[i] for i in range(4)], "x", BF16)
    first = ring_scatter([first[i] for i in range(4)], "x", F32)
    second = ring_scatter([second[i] for i in range(4)], "y", F32)

    left = depth - first.shape[0]
    grad_in = jnp.concatenate([first, second[:left]], 0)
    packed = second[left:]
    grad_down = jnp.concatenate([packed[:, i * depth : (i + 1) * depth] for i in range(3)], 0)

    gg = gg.reshape(y_size, pairs, 2, block).transpose(1, 2, 0, 3).reshape(z_size, y_size, block)
    gg = jnp.sum(jnp.where(hit, gg[:, :, None], 0.0), 1)
    gg = jnp.stack([gg[DISTANCES.index(d)] for d in range(z_size)])
    for by in (4, 2, 1):
        gg = gg[:by] + shift(gg[by:], "z", -by)
    return mixed_out, gg[0].T, grad_in[None], grad_down[None]


def solution(mesh):
    wide = Mesh(mesh.devices.reshape(4, 2, 8, 4), ("x", "core", "z", "y"))
    rows = P(("x", "core", "z", "y"), None)
    expert = P(("z", "y"), None, None)
    return jax.shard_map(
        on_device,
        mesh=wide,
        in_specs=(rows, rows, rows, rows, expert, expert),
        out_specs=(
            rows,
            rows,
            P(("z", "y"), ("x", "core"), None),
            P(("z", "y"), None, ("x", "core")),
        ),
        check_vma=False,
    )
```

```python
import jax
import jax.numpy as jnp
from jax import lax
from jax.experimental import pallas as pl
from jax.experimental.pallas import tpu as pltpu
from jax.sharding import Mesh, PartitionSpec as P

BF16 = jnp.bfloat16
F32 = jnp.float32
VMEM_BYTES = 48 * 1024 * 1024
SLOTS = 80
PAIRS = ((1, 7), (2, 6), (3, 5), (0, 4))
DISTANCES = tuple(d for pair in PAIRS for d in pair)


def params(steps=1):
    return pltpu.CompilerParams(
        dimension_semantics=("arbitrary",) * steps, vmem_limit_bytes=VMEM_BYTES
    )


def cost(flops, moved):
    return pl.CostEstimate(flops=flops, bytes_accessed=moved, transcendentals=0)


def chosen(slot_row):
    tokens = slot_row.shape[1]
    return lax.broadcasted_iota(jnp.int32, (SLOTS, tokens), 0) == slot_row


def select_kernel(count, *refs):
    slot_ref, pieces, out_ref, rows_ref = refs[0], refs[1 : 1 + count], refs[-2], refs[-1]
    experts = slot_ref.shape[1]
    at = 0
    for piece in pieces:
        rows_ref[at : at + piece.shape[0], :] = piece[...]
        at += piece.shape[0]
    pick = jnp.concatenate(
        [chosen(slot_ref[0, e : e + 1, :]).astype(BF16) for e in range(experts)], 0
    )
    width = rows_ref.shape[1]
    for n in range(0, width, 512):
        got = jnp.dot(pick, rows_ref[:, n : n + 512], preferred_element_type=F32).astype(BF16)
        out_ref[:, 0, :, n : n + 512] = got.reshape(experts, SLOTS, 512)


def select(pair, slots, pieces, buffer):
    pairs, experts, tokens = slots.shape
    width = pieces[0].shape[1]
    operands = [slots, *pieces]
    in_specs = [pl.BlockSpec((1, experts, tokens), lambda i: (pair, 0, 0))]
    in_specs += [pl.BlockSpec(piece.shape, lambda i: (0, 0)) for piece in pieces]
    aliases = {}
    if buffer is not None:
        aliases = {len(operands): 0}
        operands.append(buffer)
        in_specs.append(pl.BlockSpec(memory_space=pl.ANY))
    count = len(pieces)
    return pl.pallas_call(
        lambda *refs: select_kernel(count, *refs),
        grid=(1,),
        in_specs=in_specs,
        out_specs=pl.BlockSpec((experts, 1, SLOTS, width), lambda i: (0, pair, 0, 0)),
        out_shape=jax.ShapeDtypeStruct((experts, pairs, SLOTS, width), BF16),
        scratch_shapes=[pltpu.VMEM((tokens, width), BF16)],
        input_output_aliases=aliases,
        compiler_params=params(),
        cost_estimate=cost(2 * experts * SLOTS * tokens * width, 3 << 20),
    )(*operands)


def forward_kernel(place_ref, x_ref, w_ref, silu_ref, slope_ref, hidden_ref):
    width = x_ref.shape[2]
    hidden = hidden_ref.shape[2]
    w = w_ref[...].reshape(width, 2 * hidden)
    pre = jnp.dot(x_ref[0], w, preferred_element_type=F32)
    gate_pre, up_pre = pre[:, :hidden], pre[:, hidden:]
    sig = jax.nn.sigmoid(gate_pre)
    silu = gate_pre * sig
    silu_ref[0] = silu.astype(BF16)
    slope_ref[0] = (up_pre * sig * (1.0 + gate_pre * (1.0 - sig))).astype(BF16)
    hidden_ref[0] = (silu * up_pre).astype(BF16)


def forward(place, x, w_in_all):
    experts, rows, width = x.shape
    shares, _, depth, columns = w_in_all.shape
    hidden = columns // 2
    out = jax.ShapeDtypeStruct((experts, rows, hidden), BF16)
    spec = pl.BlockSpec((1, rows, hidden), lambda e, p: (e, 0, 0))
    return pl.pallas_call(
        forward_kernel,
        grid_spec=pltpu.PrefetchScalarGridSpec(
            num_scalar_prefetch=1,
            grid=(experts,),
            in_specs=[
                pl.BlockSpec((1, rows, width), lambda e, p: (e, 0, 0)),
                pl.BlockSpec((shares, 1, depth, columns), lambda e, p: (0, p[e], 0, 0)),
            ],
            out_specs=[spec] * 3,
        ),
        out_shape=[out] * 3,
        compiler_params=params(),
        cost_estimate=cost(2 * rows * width * columns * experts, 21 << 20),
    )(place, x, w_in_all)


def hidden_kernel(
    core_ref, c_ref, w_ref, slot_ref, gate_ref, silu_ref, slope_ref, hidden_ref,
    pre_ref, hst_ref, y_ref, gg_ref,
):
    rows, width = c_ref.shape[1:]
    hidden = hidden_ref.shape[2]
    half = width // 2
    pairs = slot_ref.shape[1]
    own = pl.ds(pl.multiple_of(core_ref[0] * half, half), half)
    other = pl.ds(pl.multiple_of((1 - core_ref[0]) * half, half), half)
    across = (((1,), (1,)), ((), ()))
    raw = lax.dot_general(c_ref[0, :, own], w_ref[0, 0], across, preferred_element_type=F32)
    raw += lax.dot_general(c_ref[0, :, other], w_ref[0, 1], across, preferred_element_type=F32)
    picks = [chosen(slot_ref[0, p : p + 1, :]) for p in range(pairs)]
    gate = jnp.concatenate(
        [
            jnp.sum(jnp.where(picks[p], gate_ref[0, p : p + 1, :], 0.0), 1, keepdims=True)
            for p in range(pairs)
        ],
        0,
    )
    act = hidden_ref[0]
    for part, at in ((0, own), (1, other)):
        out = jnp.dot(act, w_ref[0, part], preferred_element_type=F32)
        y_ref[0, :, at] = (out * gate).astype(BF16)
    act = act.astype(F32)
    inner = jnp.sum(act * raw, 1, keepdims=True)
    for p in range(pairs):
        gg_ref[0, p : p + 1, :] = jnp.sum(
            jnp.where(picks[p], inner[p * SLOTS : (p + 1) * SLOTS], 0.0), 0, keepdims=True
        )
    hst_ref[0] = (act * gate).astype(BF16).T
    grad = raw * gate
    pre_ref[0, :, :hidden] = (grad * slope_ref[0].astype(F32)).astype(BF16)
    pre_ref[0, :, hidden:] = (grad * silu_ref[0].astype(F32)).astype(BF16)


def hidden_gradient(core, c, w_down_all, slots, gates, silu, slope, act):
    experts, rows, width = c.shape
    hidden = w_down_all.shape[2]
    _, pairs, tokens = slots.shape
    one = lambda *shape: pl.BlockSpec((1, *shape), lambda e, p: (e,) + (0,) * len(shape))
    wide = one(rows, hidden)
    return pl.pallas_call(
        hidden_kernel,
        grid_spec=pltpu.PrefetchScalarGridSpec(
            num_scalar_prefetch=1,
            grid=(experts,),
            in_specs=[
                one(rows, width),
                one(2, hidden, width // 2),
                one(pairs, tokens),
                one(pairs, tokens),
                wide,
                wide,
                wide,
            ],
            out_specs=[
                one(rows, 2 * hidden),
                one(hidden, rows),
                one(rows, width),
                one(pairs, tokens),
            ],
        ),
        out_shape=[
            jax.ShapeDtypeStruct((experts, rows, 2 * hidden), BF16),
            jax.ShapeDtypeStruct((experts, hidden, rows), BF16),
            jax.ShapeDtypeStruct((experts, rows, width), BF16),
            jax.ShapeDtypeStruct((experts, pairs, tokens), F32),
        ],
        compiler_params=params(),
        cost_estimate=cost(4 * rows * width * hidden * experts, 23 << 20),
    )(core, c, w_down_all, slots, gates, silu, slope, act)


def output_kernel(place_ref, slot_ref, y_ref, *refs):
    out_ref, pick_ref = refs[-2:]
    pairs, experts, tokens = slot_ref.shape
    block = tokens // 2
    columns = out_ref.shape[2]

    @pl.when(pl.program_id(0) == 0)
    def _():
        for p in range(pairs):
            pick = jnp.concatenate(
                [chosen(slot_ref[p, e : e + 1, :]).astype(BF16) for e in range(experts)], 0
            )
            pick_ref[p] = pick.T

    for p in range(pairs):
        y = y_ref[:, p].reshape(experts * SLOTS, columns)
        total = jnp.dot(pick_ref[p], y, preferred_element_type=F32).astype(BF16)
        for j in range(2):
            out_ref[pl.ds(place_ref[2 * p + j], 1)] = total[j * block : (j + 1) * block].reshape(
                1, block, columns
            )


def output_rows(place, slots, y, after):
    pairs, experts, tokens = slots.shape
    width = y.shape[3]
    columns = 512
    return pl.pallas_call(
        output_kernel,
        grid_spec=pltpu.PrefetchScalarGridSpec(
            num_scalar_prefetch=1,
            grid=(width // columns,),
            in_specs=[
                pl.BlockSpec((pairs, experts, tokens), lambda n, p: (0, 0, 0)),
                pl.BlockSpec((experts, pairs, SLOTS, columns), lambda n, p: (0, 0, 0, n)),
            ]
            + [pl.BlockSpec(memory_space=pl.ANY)] * len(after),
            out_specs=pl.BlockSpec((2 * pairs, tokens // 2, columns), lambda n, p: (0, 0, n)),
            scratch_shapes=[pltpu.VMEM((pairs, tokens, experts * SLOTS), BF16)],
        ),
        out_shape=jax.ShapeDtypeStruct((2 * pairs, tokens // 2, width), BF16),
        compiler_params=params(),
        cost_estimate=cost(2 * pairs * experts * SLOTS * tokens * width, 10 << 20),
    )(place, slots, y, *after)


def weight_kernel(more, place_ref, xa_ref, pa_ref, xb_ref, cb_ref, pb_ref, hb_ref, *refs):
    first_ref, second_ref = refs[-2:]
    columns = pa_ref.shape[2]
    hidden = hb_ref.shape[1]
    share = xa_ref.shape[2]
    half = first_ref.shape[2]
    piece = hidden // 3
    first = jnp.dot(xa_ref[0].T[:half], pa_ref[0], preferred_element_type=F32)
    rest = jnp.dot(xb_ref[0].T[half:], pb_ref[0], preferred_element_type=F32)
    down = jnp.dot(hb_ref[0], cb_ref[0], preferred_element_type=F32)
    packed = jnp.concatenate([down[i * piece : (i + 1) * piece] for i in range(3)], 1)
    second = jnp.concatenate([rest, packed], 0)
    if more:
        first += refs[0][0, 0].astype(F32)
        second += refs[1][0, 0].astype(F32)
    first_ref[0, 0] = first.astype(BF16)
    second_ref[0, 0] = second.astype(BF16)


def weight_gradient(base, place, x, c, pre, hst, ring, other, after):
    experts, rows, columns = pre.shape
    hidden = hst.shape[1]
    share = x.shape[2] // (2 * ring)
    half = (share + hidden // 3) // 2
    count = 2 if base == 1 else 1
    out = jax.ShapeDtypeStruct((count, ring, half, columns), BF16)
    part = pl.BlockSpec((1, 1, half, columns), lambda n, s, p: (n, s, 0, 0))
    more = bool(other)
    return pl.pallas_call(
        lambda *refs: weight_kernel(more, *refs),
        grid_spec=pltpu.PrefetchScalarGridSpec(
            num_scalar_prefetch=1,
            grid=(count, ring),
            in_specs=[
                pl.BlockSpec((1, rows, share), lambda n, s, p: (base + 2 * n, 0, p[s])),
                pl.BlockSpec((1, rows, columns), lambda n, s, p: (base + 2 * n, 0, 0)),
                pl.BlockSpec((1, rows, share), lambda n, s, p: (s, 0, p[base + 2 * n])),
                pl.BlockSpec((1, rows, share), lambda n, s, p: (s, 0, p[base + 2 * n])),
                pl.BlockSpec((1, rows, columns), lambda n, s, p: (s, 0, 0)),
                pl.BlockSpec((1, hidden, rows), lambda n, s, p: (s, 0, 0)),
            ]
            + [part, part] * more
            + [pl.BlockSpec(memory_space=pl.ANY)] * len(after),
            out_specs=[part, part],
        ),
        out_shape=[out, out],
        compiler_params=params(2),
        cost_estimate=cost(rows * x.shape[2] * 3 * hidden * count, 7 * count << 20),
    )(place, x, pre, x, c, pre, hst, *other, *after)


def join_kernel(low_ref, high_ref, *refs):
    count = low_ref.shape[0]
    refs[-1][:count] = low_ref[...]
    refs[-1][count:] = high_ref[...]


def join(low, high, after):
    whole = pl.BlockSpec(low.shape, lambda i: (0, 0, 0))
    shape = (2 * low.shape[0], *low.shape[1:])
    return pl.pallas_call(
        join_kernel,
        grid=(1,),
        in_specs=[whole, whole] + [pl.BlockSpec(memory_space=pl.ANY)] * len(after),
        out_specs=pl.BlockSpec(shape, lambda i: (0, 0, 0)),
        out_shape=jax.ShapeDtypeStruct(shape, low.dtype),
        compiler_params=pltpu.CompilerParams(vmem_limit_bytes=8 * 1024 * 1024),
        cost_estimate=cost(0, 1 << 17),
    )(low, high, *after)


def shift(value, axis, by):
    n = lax.axis_size(axis)
    return lax.ppermute(value, axis, [(i, (i + by) % n) for i in range(n)])


def ring_step(held, axis):
    below, above = held
    return shift(below, axis, 1), shift(above, axis, -1)


def add(*terms):
    total = terms[0].astype(F32)
    for term in terms[1:]:
        total = total + term.astype(F32)
    return total


def ring_scatter(parts, axis, kind):
    half = parts[0].shape[0] // 2
    low = shift(parts[2][:half], axis, 1)
    high = shift(parts[2][half:], axis, -1)
    to_up = jnp.concatenate([add(parts[1][:half], low).astype(BF16), parts[1][half:]], 0)
    to_down = jnp.concatenate([parts[3][:half], add(parts[3][half:], high).astype(BF16)], 0)
    low, high = shift(to_up, axis, 1), shift(to_down, axis, -1)
    return add(parts[0], low, high).astype(kind)


def swap_cores(value):
    return lax.ppermute(value, "core", [(0, 1), (1, 0)])


def on_device(tokens, gates, routes, cotangent, w_in, w_down):
    block, width = tokens.shape
    hidden = w_down.shape[1]
    top = routes.shape[1]
    x_at, core_at = lax.axis_index("x"), lax.axis_index("core")
    z_at, y_at = lax.axis_index("z"), lax.axis_index("y")
    z_size, y_size = lax.axis_size("z"), lax.axis_size("y")
    pairs = len(PAIRS)
    experts_at = jnp.remainder(y_at + jnp.arange(y_size), y_size).astype(jnp.int32)

    depth = width // 8
    share_in = lax.dynamic_slice_in_dim(w_in[0], (x_at * 2 + core_at) * depth, depth, 0)
    w_in_all = lax.all_gather(share_in, ("x", "core", "y"), axis=0, tiled=True)
    w_in_all = w_in_all.reshape(8, y_size, depth, 2 * hidden)

    small = jnp.concatenate([routes.T.astype(F32), gates.T], 0)[None]
    order = [0]
    held = {"tokens": (tokens, tokens), "cot": (cotangent, cotangent)}
    got = {name: {0: [both[0]]} for name, both in held.items()}
    for step, by in ((1, 4), (2, 2), (3, 1)):
        held = {name: ring_step(both, "z") for name, both in held.items()}
        for name, (below, above) in held.items():
            got[name][step], got[name][z_size - step] = [below], [above]
        after = [one for both in held.values() for one in both] if step < 3 else []
        small = join(small, shift(small, "z", by), after)
        order += [o + by for o in order]
    for name, (below, above) in held.items():
        got[name][4] = [
            shift(below[: block // 2], "z", 1), shift(above[block // 2 :], "z", -1)
        ]
    small = jnp.stack([small[order.index(d)] for d in DISTANCES])
    ring_routes, ring_gates = small[:, :top].astype(jnp.int32), small[:, top:]
    hit = ring_routes[:, None] == (z_at * y_size + experts_at)[None, :, None, None]
    gate_of = jnp.sum(jnp.where(hit, ring_gates[:, None], 0.0), 2)
    any_hit = jnp.any(hit, 2)
    earlier = jnp.arange(block)[:, None] < jnp.arange(block)[None, :]
    slot = jnp.dot(
        any_hit.reshape(-1, block).astype(BF16), earlier.astype(BF16), preferred_element_type=F32
    )
    slot = slot.reshape(pairs, 2, y_size, block).astype(jnp.int32)
    slot = slot + (SLOTS // 2) * jnp.arange(2, dtype=jnp.int32)[None, :, None, None]
    slot = jnp.where(any_hit.reshape(slot.shape), slot, -1)
    slots = jnp.swapaxes(slot, 1, 2).reshape(pairs, y_size, 2 * block)
    expert_slots = jnp.swapaxes(slots, 0, 1)
    gate_of = gate_of.reshape(pairs, 2, y_size, block).transpose(2, 0, 1, 3)
    gate_of = gate_of.reshape(y_size, pairs, 2 * block)

    half = width // 2
    own = lax.dynamic_slice_in_dim(w_down[0], core_at * half, half, 1)
    rest = lax.dynamic_slice_in_dim(w_down[0], (1 - core_at) * half, half, 1)
    below, above = shift(own, "y", 1), shift(own, "y", -1)
    cut = hidden // 2
    far = jnp.concatenate([shift(below[:cut], "y", 1), shift(above[cut:], "y", -1)], 0)
    w_down_all = jnp.stack(
        [jnp.stack([own, rest])]
        + [jnp.stack([held, swap_cores(held)]) for held in (above, far, below)]
    )

    def routed(pieces):
        buffer = None
        for p, (a, b) in enumerate(PAIRS):
            buffer = select(p, slots, pieces[a] + pieces[b], buffer)
        return buffer.reshape(y_size, pairs * SLOTS, width)

    rows_in = routed(got["tokens"])
    rows_cot = routed(got["cot"])
    silu, slope, act = forward(experts_at, rows_in, w_in_all)
    pre, hst, y, gg = hidden_gradient(
        core_at.astype(jnp.int32)[None], rows_cot, w_down_all, expert_slots, gate_of,
        silu, slope, act,
    )

    shares_at = jnp.remainder(x_at + jnp.arange(4), 4).astype(jnp.int32) * 2
    place = jnp.remainder(z_at - jnp.array(DISTANCES), z_size).astype(jnp.int32)

    def grads(base, core, other, after):
        return weight_gradient(
            base, shares_at + core, rows_in, rows_cot, pre, hst, 4, other, after
        )

    theirs_2 = grads(2, 1 - core_at, [], [])
    theirs_1 = grads(1, 1 - core_at, [], theirs_2[:1])
    ours_2 = grads(2, core_at, [swap_cores(g) for g in theirs_2], theirs_1[:1])
    partial = output_rows(
        place, slots, y.reshape(y_size, pairs, SLOTS, width), ours_2[:1]
    )
    mixed_out = lax.psum_scatter(partial, "z", scatter_dimension=0, tiled=True)[0]
    theirs_0 = grads(0, 1 - core_at, [], [partial])
    ours_1 = grads(1, core_at, [swap_cores(g) for g in theirs_1], theirs_0[:1])
    ours_0 = grads(0, core_at, [swap_cores(g) for g in theirs_0], ours_1[:1])
    first, second = [
        [near[0], between[0], far[0], between[1]]
        for near, between, far in zip(ours_0, ours_1, ours_2)
    ]
    first = ring_scatter(first, "y", BF16)
    second = ring_scatter(second, "x", BF16)
    first = ring_scatter([first[i] for i in range(4)], "x", F32)
    second = ring_scatter([second[i] for i in range(4)], "y", F32)

    left = depth - first.shape[0]
    grad_in = jnp.concatenate([first, second[:left]], 0)
    packed = second[left:]
    grad_down = jnp.concatenate([packed[:, i * depth : (i + 1) * depth] for i in range(3)], 0)

    gg = gg.reshape(y_size, pairs, 2, block).transpose(1, 2, 0, 3).reshape(z_size, y_size, block)
    gg = jnp.sum(jnp.where(hit, gg[:, :, None], 0.0), 1)
    gg = jnp.stack([gg[DISTANCES.index(d)] for d in range(z_size)])
    for by in (4, 2, 1):
        gg = gg[:by] + shift(gg[by:], "z", -by)
    return mixed_out, gg[0].T, grad_in[None], grad_down[None]


def solution(mesh):
    wide = Mesh(mesh.devices.reshape(4, 2, 8, 4), ("x", "core", "z", "y"))
    rows = P(("x", "core", "z", "y"), None)
    expert = P(("z", "y"), None, None)
    return jax.shard_map(
        on_device,
        mesh=wide,
        in_specs=(rows, rows, rows, rows, expert, expert),
        out_specs=(
            rows,
            rows,
            P(("z", "y"), ("x", "core"), None),
            P(("z", "y"), None, ("x", "core")),
        ),
        check_vma=False,
    )
```

```python
import jax
import jax.numpy as jnp
from jax import lax
from jax.experimental import pallas as pl
from jax.experimental.pallas import tpu as pltpu
from jax.sharding import Mesh, PartitionSpec as P

BF16 = jnp.bfloat16
F32 = jnp.float32
VMEM_BYTES = 48 * 1024 * 1024
SLOTS = 80
PAIRS = ((1, 7), (2, 6), (3, 5), (0, 4))
DISTANCES = tuple(d for pair in PAIRS for d in pair)


def params(steps=1):
    return pltpu.CompilerParams(
        dimension_semantics=("arbitrary",) * steps, vmem_limit_bytes=VMEM_BYTES
    )


def cost(flops, moved):
    return pl.CostEstimate(flops=flops, bytes_accessed=moved, transcendentals=0)


def chosen(slot_row):
    tokens = slot_row.shape[1]
    return lax.broadcasted_iota(jnp.int32, (SLOTS, tokens), 0) == slot_row


def select_kernel(count, core_ref, slot_ref, *refs):
    pieces, rows_ref = refs[:count], refs[-1]
    outs = refs[-3], refs[-2]
    experts = slot_ref.shape[1]
    at = 0
    for piece in pieces:
        rows_ref[at : at + piece.shape[0], :] = piece[...]
        at += piece.shape[0]
    pick = jnp.concatenate(
        [chosen(slot_ref[0, e : e + 1, :]).astype(BF16) for e in range(experts)], 0
    )
    share = outs[0].shape[3] // 4
    for part, out_ref in enumerate(outs):
        core = core_ref[0] if part == 0 else 1 - core_ref[0]
        for i in range(4):
            at = pl.ds(pl.multiple_of((2 * i + core) * share, share), share)
            got = jnp.dot(pick, rows_ref[:, at], preferred_element_type=F32).astype(BF16)
            out_ref[:, 0, :, i * share : (i + 1) * share] = got.reshape(experts, SLOTS, share)


def select(pair, core, slots, pieces, buffers):
    pairs, experts, tokens = slots.shape
    width = pieces[0][0].shape[1]
    operands = [core, slots, *(array for array, _ in pieces)]
    in_specs = [pl.BlockSpec((1, experts, tokens), lambda i, c: (pair, 0, 0))]
    in_specs += [
        pl.BlockSpec((tokens // 2, width), lambda i, c, at=at: (at, 0)) for _, at in pieces
    ]
    aliases = {}
    if buffers:
        aliases = {len(operands) + i: i for i in range(2)}
        operands += buffers
        in_specs += [pl.BlockSpec(memory_space=pl.ANY)] * 2
    count = len(pieces)
    out = jax.ShapeDtypeStruct((experts, pairs, SLOTS, width // 2), BF16)
    return pl.pallas_call(
        lambda *refs: select_kernel(count, *refs),
        grid_spec=pltpu.PrefetchScalarGridSpec(
            num_scalar_prefetch=1,
            grid=(1,),
            in_specs=in_specs,
            out_specs=[
                pl.BlockSpec((experts, 1, SLOTS, width // 2), lambda i, c: (0, pair, 0, 0))
            ]
            * 2,
            scratch_shapes=[pltpu.VMEM((tokens, width), BF16)],
        ),
        out_shape=[out, out],
        input_output_aliases=aliases,
        compiler_params=params(),
        cost_estimate=cost(2 * experts * SLOTS * tokens * width, 3 << 20),
    )(*operands)


def forward_kernel(place_ref, own_ref, other_ref, w_own_ref, w_other_ref, *refs):
    silu_ref, slope_ref, hidden_ref = refs
    half = own_ref.shape[2]
    hidden = hidden_ref.shape[2]
    pre = jnp.dot(
        own_ref[0], w_own_ref[...].reshape(half, 2 * hidden), preferred_element_type=F32
    )
    pre += jnp.dot(
        other_ref[0], w_other_ref[...].reshape(half, 2 * hidden), preferred_element_type=F32
    )
    gate_pre, up_pre = pre[:, :hidden], pre[:, hidden:]
    sig = jax.nn.sigmoid(gate_pre)
    silu = gate_pre * sig
    silu_ref[0] = silu.astype(BF16)
    slope_ref[0] = (up_pre * sig * (1.0 + gate_pre * (1.0 - sig))).astype(BF16)
    hidden_ref[0] = (silu * up_pre).astype(BF16)


def forward(place, rows_in, w_in_all):
    experts, rows, half = rows_in[0].shape
    x_size, _, _, depth, columns = w_in_all.shape
    hidden = columns // 2
    out = jax.ShapeDtypeStruct((experts, rows, hidden), BF16)
    spec = pl.BlockSpec((1, rows, hidden), lambda e, p: (e, 0, 0))
    row_spec = pl.BlockSpec((1, rows, half), lambda e, p: (e, 0, 0))
    weights = (x_size, 1, 1, depth, columns)
    return pl.pallas_call(
        forward_kernel,
        grid_spec=pltpu.PrefetchScalarGridSpec(
            num_scalar_prefetch=1,
            grid=(experts,),
            in_specs=[
                row_spec,
                row_spec,
                pl.BlockSpec(weights, lambda e, p: (0, p[4], p[e], 0, 0)),
                pl.BlockSpec(weights, lambda e, p: (0, 1 - p[4], p[e], 0, 0)),
            ],
            out_specs=[spec] * 3,
        ),
        out_shape=[out] * 3,
        compiler_params=params(),
        cost_estimate=cost(4 * rows * half * columns * experts, 21 << 20),
    )(place, *rows_in, w_in_all, w_in_all)


def hidden_kernel(
    core_ref, own_ref, other_ref, w_ref, slot_ref, gate_ref, silu_ref, slope_ref, hidden_ref,
    pre_ref, hs_ref, y_ref, gg_ref,
):
    hidden = hidden_ref.shape[2]
    share = own_ref.shape[2] // 4
    pairs = slot_ref.shape[1]
    across = (((1,), (1,)), ((), ()))
    raw = lax.dot_general(own_ref[0], w_ref[0, 0], across, preferred_element_type=F32)
    raw += lax.dot_general(other_ref[0], w_ref[0, 1], across, preferred_element_type=F32)
    picks = [chosen(slot_ref[0, p : p + 1, :]) for p in range(pairs)]
    gate = jnp.concatenate(
        [
            jnp.sum(jnp.where(picks[p], gate_ref[0, p : p + 1, :], 0.0), 1, keepdims=True)
            for p in range(pairs)
        ],
        0,
    )
    act = hidden_ref[0]
    for part in range(2):
        out = jnp.dot(act, w_ref[0, part], preferred_element_type=F32)
        out = (out * gate).astype(BF16)
        core = core_ref[0] if part == 0 else 1 - core_ref[0]
        for i in range(4):
            at = pl.ds(pl.multiple_of((2 * i + core) * share, share), share)
            y_ref[0, :, at] = out[:, i * share : (i + 1) * share]
    act = act.astype(F32)
    inner = jnp.sum(act * raw, 1, keepdims=True)
    for p in range(pairs):
        gg_ref[0, p : p + 1, :] = jnp.sum(
            jnp.where(picks[p], inner[p * SLOTS : (p + 1) * SLOTS], 0.0), 0, keepdims=True
        )
    hs_ref[0] = (act * gate).astype(BF16)
    grad = raw * gate
    pre_ref[0, :, :hidden] = (grad * slope_ref[0].astype(F32)).astype(BF16)
    pre_ref[0, :, hidden:] = (grad * silu_ref[0].astype(F32)).astype(BF16)


def hidden_gradient(core, rows_cot, w_down_all, slots, gates, silu, slope, act):
    experts, rows, half = rows_cot[0].shape
    hidden = w_down_all.shape[2]
    _, pairs, tokens = slots.shape
    one = lambda *shape: pl.BlockSpec((1, *shape), lambda e, p: (e,) + (0,) * len(shape))
    wide = one(rows, hidden)
    return pl.pallas_call(
        hidden_kernel,
        grid_spec=pltpu.PrefetchScalarGridSpec(
            num_scalar_prefetch=1,
            grid=(experts,),
            in_specs=[
                one(rows, half),
                one(rows, half),
                one(2, hidden, half),
                one(pairs, tokens),
                one(pairs, tokens),
                wide,
                wide,
                wide,
            ],
            out_specs=[
                one(rows, 2 * hidden),
                wide,
                one(rows, 2 * half),
                one(pairs, tokens),
            ],
        ),
        out_shape=[
            jax.ShapeDtypeStruct((experts, rows, 2 * hidden), BF16),
            jax.ShapeDtypeStruct((experts, rows, hidden), BF16),
            jax.ShapeDtypeStruct((experts, rows, 2 * half), BF16),
            jax.ShapeDtypeStruct((experts, pairs, tokens), F32),
        ],
        compiler_params=params(),
        cost_estimate=cost(8 * rows * half * hidden * experts, 23 << 20),
    )(core, *rows_cot, w_down_all, slots, gates, silu, slope, act)


def shares_kernel(core_ref, w_own_ref, w_other_ref, own_ref, other_ref):
    own_ref[...] = w_own_ref[0]
    other_ref[...] = w_other_ref[0]


def column_shares(core, w, share):
    _, rows, width = w.shape
    out = jax.ShapeDtypeStruct((rows, width // 2), w.dtype)
    return pl.pallas_call(
        shares_kernel,
        grid_spec=pltpu.PrefetchScalarGridSpec(
            num_scalar_prefetch=1,
            grid=(width // (2 * share),),
            in_specs=[
                pl.BlockSpec((1, rows, share), lambda i, c: (0, 0, 2 * i + c[0])),
                pl.BlockSpec((1, rows, share), lambda i, c: (0, 0, 2 * i + 1 - c[0])),
            ],
            out_specs=[pl.BlockSpec((rows, share), lambda i, c: (0, i))] * 2,
        ),
        out_shape=[out, out],
        compiler_params=params(),
        cost_estimate=cost(0, 3 << 20),
    )(core, w, w)


def output_kernel(place_ref, slot_ref, y_ref, out_ref, pick_ref):
    pairs, experts, tokens = slot_ref.shape
    block = tokens // 2
    columns = out_ref.shape[2]

    @pl.when(pl.program_id(0) == 0)
    def _():
        for p in range(pairs):
            pick = jnp.concatenate(
                [chosen(slot_ref[p, e : e + 1, :]).astype(BF16) for e in range(experts)], 0
            )
            pick_ref[p] = pick.T

    for p in range(pairs):
        y = y_ref[:, p].reshape(experts * SLOTS, columns)
        total = jnp.dot(pick_ref[p], y, preferred_element_type=F32).astype(BF16)
        for j in range(2):
            out_ref[pl.ds(place_ref[2 * p + j], 1)] = total[j * block : (j + 1) * block].reshape(
                1, block, columns
            )


def output_rows(place, slots, y):
    pairs, experts, tokens = slots.shape
    width = y.shape[3]
    columns = 512
    return pl.pallas_call(
        output_kernel,
        grid_spec=pltpu.PrefetchScalarGridSpec(
            num_scalar_prefetch=1,
            grid=(width // columns,),
            in_specs=[
                pl.BlockSpec((pairs, experts, tokens), lambda n, p: (0, 0, 0)),
                pl.BlockSpec((experts, pairs, SLOTS, columns), lambda n, p: (0, 0, 0, n)),
            ],
            out_specs=pl.BlockSpec((2 * pairs, tokens // 2, columns), lambda n, p: (0, 0, n)),
            scratch_shapes=[pltpu.VMEM((pairs, tokens, experts * SLOTS), BF16)],
        ),
        out_shape=jax.ShapeDtypeStruct((2 * pairs, tokens // 2, width), BF16),
        compiler_params=params(),
        cost_estimate=cost(2 * pairs * experts * SLOTS * tokens * width, 10 << 20),
    )(place, slots, y)


def weight_kernel(place_ref, *refs):
    (x, c, pre, hs), (x2, c2, pre2, hs2) = refs[:4], refs[4:8]
    first_ref, second_ref = refs[8:]
    columns = pre.shape[2]
    hidden = hs.shape[2]
    ring, _, half, _ = second_ref.shape
    share = x.shape[2] // ring
    piece = hidden // 3
    hst, hst2 = hs[0].T, hs2[0].T
    for i in range(ring):
        at = slice(i * share, (i + 1) * share)
        grad_in = jnp.dot(x[0, :, at].T, pre[0], preferred_element_type=F32)
        grad_in += jnp.dot(x2[0, :, at].T, pre2[0], preferred_element_type=F32)
        down = jnp.dot(hst, c[0, :, at], preferred_element_type=F32)
        down += jnp.dot(hst2, c2[0, :, at], preferred_element_type=F32)
        to = pl.ds(place_ref[i], 1)
        first_ref[0, to] = grad_in[:half].astype(BF16).reshape(1, half, columns)
        packed = jnp.concatenate([down[n * piece : (n + 1) * piece] for n in range(3)], 1)
        second_ref[to, 0] = (
            jnp.concatenate([grad_in[half:], packed], 0).astype(BF16).reshape(1, half, columns)
        )


def weight_gradient(place, ours, theirs):
    x, _, pre, hs = ours
    experts, rows, columns = pre.shape
    hidden = hs.shape[2]
    ring = 4
    half = (x.shape[2] // ring + hidden // 3) // 2
    one = lambda *shape: pl.BlockSpec((1, *shape), lambda e, p: (e,) + (0,) * len(shape))
    specs = [one(*value.shape[1:]) for value in ours]
    return pl.pallas_call(
        weight_kernel,
        grid_spec=pltpu.PrefetchScalarGridSpec(
            num_scalar_prefetch=1,
            grid=(experts,),
            in_specs=specs * 2,
            out_specs=[
                pl.BlockSpec((1, ring, half, columns), lambda e, p: (e, 0, 0, 0)),
                pl.BlockSpec((ring, 1, half, columns), lambda e, p: (0, e, 0, 0)),
            ],
        ),
        out_shape=[
            jax.ShapeDtypeStruct((experts, ring, half, columns), BF16),
            jax.ShapeDtypeStruct((ring, experts, half, columns), BF16),
        ],
        compiler_params=params(),
        cost_estimate=cost(4 * rows * x.shape[2] * 3 * hidden * experts, 26 << 20),
    )(place, *ours, *theirs)


def shift(value, axis, by):
    n = lax.axis_size(axis)
    return lax.ppermute(value, axis, [(i, (i + by) % n) for i in range(n)])


def ring_pieces(tokens, cot, axis):
    n = lax.axis_size(axis)
    both = jnp.concatenate([tokens, cot], 0)
    below = above = both
    got = {0: ((tokens, 0), (cot, 0))}
    for step in range(1, n // 2):
        below, above = shift(below, axis, 1), shift(above, axis, -1)
        got[step] = ((below, 0), (below, 1))
        got[n - step] = ((above, 0), (above, 1))
    rows = tokens.shape[0]
    got[n // 2] = ((shift(below[:rows], axis, 1), 0), (shift(above[rows:], axis, -1), 0))
    return got


def add(*terms):
    total = terms[0].astype(F32)
    for term in terms[1:]:
        total = total + term.astype(F32)
    return total


def ring_scatter(parts, axis, kind):
    half = parts[0].shape[0] // 2
    low = shift(parts[2][:half], axis, 1)
    high = shift(parts[2][half:], axis, -1)
    to_up = jnp.concatenate([add(parts[1][:half], low).astype(BF16), parts[1][half:]], 0)
    to_down = jnp.concatenate([parts[3][:half], add(parts[3][half:], high).astype(BF16)], 0)
    low, high = shift(to_up, axis, 1), shift(to_down, axis, -1)
    return add(parts[0], low, high).astype(kind)


def swap_cores(value):
    return lax.ppermute(value, "core", [(0, 1), (1, 0)])


def on_device(tokens, gates, routes, cotangent, w_in, w_down):
    block, width = tokens.shape
    hidden = w_down.shape[1]
    top = routes.shape[1]
    x_at, core_at = lax.axis_index("x"), lax.axis_index("core")
    z_at, y_at = lax.axis_index("z"), lax.axis_index("y")
    z_size, y_size = lax.axis_size("z"), lax.axis_size("y")
    pairs = len(PAIRS)
    experts_at = jnp.remainder(y_at + jnp.arange(y_size), y_size).astype(jnp.int32)

    depth = width // 8
    share_in = lax.dynamic_slice_in_dim(w_in[0], (x_at * 2 + core_at) * depth, depth, 0)
    w_in_all = lax.all_gather(share_in, ("x", "core", "y"), axis=0, tiled=True)
    w_in_all = w_in_all.reshape(4, 2, y_size, depth, 2 * hidden)

    small = jnp.concatenate([routes.T.astype(F32), gates.T], 0)[None]
    order = [0]
    for by in (4, 2, 1):
        small = jnp.concatenate([small, shift(small, "z", by)], 0)
        order += [o + by for o in order]
    small = jnp.stack([small[order.index(d)] for d in DISTANCES])
    ring_routes, ring_gates = small[:, :top].astype(jnp.int32), small[:, top:]
    hit = ring_routes[:, None] == (z_at * y_size + experts_at)[None, :, None, None]
    gate_of = jnp.sum(jnp.where(hit, ring_gates[:, None], 0.0), 2)
    any_hit = jnp.any(hit, 2)
    earlier = jnp.arange(block)[:, None] < jnp.arange(block)[None, :]
    slot = jnp.dot(
        any_hit.reshape(-1, block).astype(BF16), earlier.astype(BF16), preferred_element_type=F32
    )
    slot = slot.reshape(pairs, 2, y_size, block).astype(jnp.int32)
    slot = slot + (SLOTS // 2) * jnp.arange(2, dtype=jnp.int32)[None, :, None, None]
    slot = jnp.where(any_hit.reshape(slot.shape), slot, -1)
    slots = jnp.swapaxes(slot, 1, 2).reshape(pairs, y_size, 2 * block)
    expert_slots = jnp.swapaxes(slots, 0, 1)
    gate_of = gate_of.reshape(pairs, 2, y_size, block).transpose(2, 0, 1, 3)
    gate_of = gate_of.reshape(y_size, pairs, 2 * block)

    core = core_at.astype(jnp.int32)[None]
    own, rest = column_shares(core, w_down, depth)
    below, above = shift(own, "y", 1), shift(own, "y", -1)
    cut = hidden // 2
    far = jnp.concatenate([shift(below[:cut], "y", 1), shift(above[cut:], "y", -1)], 0)
    w_down_all = jnp.stack(
        [jnp.stack([own, rest])]
        + [jnp.stack([held, swap_cores(held)]) for held in (above, far, below)]
    )

    ring = ring_pieces(tokens, cotangent, "z")

    def routed(which):
        buffers = []
        for p, pair in enumerate(PAIRS):
            buffers = select(p, core, slots, [ring[d][which] for d in pair], buffers)
        return [value.reshape(y_size, pairs * SLOTS, width // 2) for value in buffers]

    rows_in, rows_cot = routed(0), routed(1)
    silu, slope, act = forward(jnp.concatenate([experts_at, core]), rows_in, w_in_all)
    pre, hs, y, gg = hidden_gradient(
        core, rows_cot, w_down_all, expert_slots, gate_of, silu, slope, act
    )
    ours = (rows_in[0], rows_cot[0], pre, hs)
    theirs = [swap_cores(value) for value in (rows_in[1], rows_cot[1], pre, hs)]
    place = jnp.remainder(z_at - jnp.array(DISTANCES), z_size).astype(jnp.int32)
    partial = output_rows(place, slots, y.reshape(y_size, pairs, SLOTS, width))
    mixed_out = lax.psum_scatter(partial, "z", scatter_dimension=0, tiled=True)[0]
    x_places = jnp.remainder(jnp.arange(4) - x_at, 4).astype(jnp.int32)
    first, second = weight_gradient(x_places, ours, theirs)
    first = ring_scatter([first[i] for i in range(4)], "y", BF16)
    second = ring_scatter([second[i] for i in range(4)], "x", BF16)
    first = ring_scatter([first[i] for i in range(4)], "x", F32)
    second = ring_scatter([second[i] for i in range(4)], "y", F32)

    left = depth - first.shape[0]
    grad_in = jnp.concatenate([first, second[:left]], 0)
    packed = second[left:]
    grad_down = jnp.concatenate([packed[:, i * depth : (i + 1) * depth] for i in range(3)], 0)

    gg = gg.reshape(y_size, pairs, 2, block).transpose(1, 2, 0, 3).reshape(z_size, y_size, block)
    gg = jnp.sum(jnp.where(hit, gg[:, :, None], 0.0), 1)
    gg = jnp.stack([gg[DISTANCES.index(d)] for d in range(z_size)])
    for by in (4, 2, 1):
        gg = gg[:by] + shift(gg[by:], "z", -by)
    return mixed_out, gg[0].T, grad_in[None], grad_down[None]


def solution(mesh):
    wide = Mesh(mesh.devices.reshape(4, 2, 8, 4), ("x", "core", "z", "y"))
    rows = P(("x", "core", "z", "y"), None)
    expert = P(("z", "y"), None, None)
    return jax.shard_map(
        on_device,
        mesh=wide,
        in_specs=(rows, rows, rows, rows, expert, expert),
        out_specs=(
            rows,
            rows,
            P(("z", "y"), ("x", "core"), None),
            P(("z", "y"), None, ("x", "core")),
        ),
        check_vma=False,
    )
```

```python
import jax
import jax.numpy as jnp
from jax import lax
from jax.experimental import pallas as pl
from jax.experimental.pallas import tpu as pltpu
from jax.sharding import Mesh, PartitionSpec as P

BF16 = jnp.bfloat16
F32 = jnp.float32
VMEM_BYTES = 48 * 1024 * 1024
SLOTS = 80
PAIRS = ((1, 7), (2, 6), (3, 5), (0, 4))
DISTANCES = tuple(d for pair in PAIRS for d in pair)
SPAN = 128
TOP = 8
LINES = 16


def params(steps=1):
    return pltpu.CompilerParams(
        dimension_semantics=("arbitrary",) * steps, vmem_limit_bytes=VMEM_BYTES
    )


def cost(flops, moved):
    return pl.CostEstimate(flops=flops, bytes_accessed=moved, transcendentals=0)


def chosen(slot_row):
    tokens = slot_row.shape[1]
    return lax.broadcasted_iota(jnp.int32, (SLOTS, tokens), 0) == slot_row


def places(meta_ref, lines_refs):
    width = lines_refs[0].shape[1]
    block = SPAN
    at = lambda ref, i: ref[
        i * block // width : i * block // width + 1, i * block % width : i * block % width + block
    ].astype(F32)
    hits, gates = [], []
    for ref in lines_refs:
        routes = [at(ref, k) for k in range(TOP)]
        parts = [at(ref, TOP + k) for k in range(3 * TOP)]
        weights = [parts[k] + parts[TOP + k] + parts[2 * TOP + k] for k in range(TOP)]
        for e in range(4):
            mine = meta_ref[1 + e].astype(F32)
            hit = jnp.zeros((1, block), F32)
            gate = jnp.zeros((1, block), F32)
            for k in range(TOP):
                same = routes[k] == mine
                hit = jnp.where(same, 1.0, hit)
                gate = jnp.where(same, weights[k], gate)
            hits.append(hit)
            gates.append(gate)
    hit = jnp.concatenate(hits, 0)
    row = lax.broadcasted_iota(jnp.int32, (block, block), 0)
    column = lax.broadcasted_iota(jnp.int32, (block, block), 1)
    earlier = jnp.where(row < column, 1.0, 0.0).astype(BF16)
    rank = jnp.dot(hit.astype(BF16), earlier, preferred_element_type=F32)
    slot = jnp.where(hit > 0.5, rank, -float(SLOTS)).astype(jnp.int32)
    slot = jnp.concatenate(
        [slot[:4], jnp.where(slot[4:] < 0, slot[4:], slot[4:] + SLOTS // 2)], 1
    )
    return slot, jnp.concatenate(
        [jnp.concatenate(gates[:4], 0), jnp.concatenate(gates[4:], 0)], 1
    )


def select_kernel(count, lines, meta_ref, *refs):
    pieces, rows_ref = refs[:count], refs[-1]
    if lines:
        slot, gate = places(meta_ref, refs[count : count + 2])
        slot_ref, gate_ref = refs[-3], refs[-2]
        slot_ref[0] = slot
        gate_ref[0] = gate
        outs = refs[-5:-3]
    else:
        slot = refs[count][0]
        outs = refs[-3:-1]
    experts = slot.shape[0]
    at = 0
    for piece in pieces:
        rows_ref[at : at + piece.shape[0], :] = piece[...]
        at += piece.shape[0]
    pick = jnp.concatenate([chosen(slot[e : e + 1]).astype(BF16) for e in range(experts)], 0)
    share = outs[0].shape[3] // 4
    for part, out_ref in enumerate(outs):
        core = meta_ref[0] if part == 0 else 1 - meta_ref[0]
        for i in range(4):
            at = pl.ds(pl.multiple_of((2 * i + core) * share, share), share)
            got = jnp.dot(pick, rows_ref[:, at], preferred_element_type=F32).astype(BF16)
            out_ref[:, 0, :, i * share : (i + 1) * share] = got.reshape(experts, SLOTS, share)


def select(pair, meta, pieces, slots, buffers):
    experts, pairs, tokens = 4, len(PAIRS), 2 * SPAN
    width = pieces[0][0].shape[1]
    operands = [meta, *(array for array, _ in pieces)]
    in_specs = [pl.BlockSpec((rows, width), lambda i, c: (0, 0)) for _, rows in pieces]
    out_shape = [jax.ShapeDtypeStruct((experts, pairs, SLOTS, width // 2), BF16)] * 2
    out_specs = [
        pl.BlockSpec((experts, 1, SLOTS, width // 2), lambda i, c: (0, pair, 0, 0))
    ] * 2
    small = pl.BlockSpec((1, experts, tokens), lambda i, c: (0, 0, 0))
    if slots is None:
        for array, rows in pieces:
            if array.shape[0] > rows:
                operands.append(array)
                in_specs.append(
                    pl.BlockSpec((LINES, width), lambda i, c, at=rows // LINES: (at, 0))
                )
        out_shape += [
            jax.ShapeDtypeStruct((1, experts, tokens), kind) for kind in (jnp.int32, F32)
        ]
        out_specs += [small, small]
    else:
        operands.append(slots)
        in_specs.append(small)
    aliases = {}
    if buffers:
        aliases = {len(operands) + i: i for i in range(2)}
        operands += buffers
        in_specs += [pl.BlockSpec(memory_space=pl.ANY)] * 2
    count = len(pieces)
    return pl.pallas_call(
        lambda *refs: select_kernel(count, slots is None, *refs),
        grid_spec=pltpu.PrefetchScalarGridSpec(
            num_scalar_prefetch=1,
            grid=(1,),
            in_specs=in_specs,
            out_specs=out_specs,
            scratch_shapes=[pltpu.VMEM((tokens, width), BF16)],
        ),
        out_shape=out_shape,
        input_output_aliases=aliases,
        compiler_params=params(),
        cost_estimate=cost(2 * experts * SLOTS * tokens * width, 3 << 20),
    )(*operands)


def forward_kernel(place_ref, own_ref, other_ref, w_own_ref, w_other_ref, *refs):
    silu_ref, slope_ref, hidden_ref = refs
    half = own_ref.shape[2]
    hidden = hidden_ref.shape[2]
    pre = jnp.dot(
        own_ref[0], w_own_ref[...].reshape(half, 2 * hidden), preferred_element_type=F32
    )
    pre += jnp.dot(
        other_ref[0], w_other_ref[...].reshape(half, 2 * hidden), preferred_element_type=F32
    )
    gate_pre, up_pre = pre[:, :hidden], pre[:, hidden:]
    sig = jax.nn.sigmoid(gate_pre)
    silu = gate_pre * sig
    silu_ref[0] = silu.astype(BF16)
    slope_ref[0] = (up_pre * sig * (1.0 + gate_pre * (1.0 - sig))).astype(BF16)
    hidden_ref[0] = (silu * up_pre).astype(BF16)


def forward(place, rows_in, w_in_all):
    experts, rows, half = rows_in[0].shape
    x_size, _, _, depth, columns = w_in_all.shape
    hidden = columns // 2
    out = jax.ShapeDtypeStruct((experts, rows, hidden), BF16)
    spec = pl.BlockSpec((1, rows, hidden), lambda e, p: (e, 0, 0))
    row_spec = pl.BlockSpec((1, rows, half), lambda e, p: (e, 0, 0))
    weights = (x_size, 1, 1, depth, columns)
    return pl.pallas_call(
        forward_kernel,
        grid_spec=pltpu.PrefetchScalarGridSpec(
            num_scalar_prefetch=1,
            grid=(experts,),
            in_specs=[
                row_spec,
                row_spec,
                pl.BlockSpec(weights, lambda e, p: (0, p[4], p[e], 0, 0)),
                pl.BlockSpec(weights, lambda e, p: (0, 1 - p[4], p[e], 0, 0)),
            ],
            out_specs=[spec] * 3,
        ),
        out_shape=[out] * 3,
        compiler_params=params(),
        cost_estimate=cost(4 * rows * half * columns * experts, 21 << 20),
    )(place, *rows_in, w_in_all, w_in_all)


def hidden_kernel(
    core_ref, own_ref, other_ref, w_ref, slot_ref, gate_ref, silu_ref, slope_ref, hidden_ref,
    pre_ref, hs_ref, y_ref, gg_ref,
):
    hidden = hidden_ref.shape[2]
    share = own_ref.shape[2] // 4
    pairs = slot_ref.shape[1]
    across = (((1,), (1,)), ((), ()))
    raw = lax.dot_general(own_ref[0], w_ref[0, 0], across, preferred_element_type=F32)
    raw += lax.dot_general(other_ref[0], w_ref[0, 1], across, preferred_element_type=F32)
    picks = [chosen(slot_ref[0, p : p + 1, :]) for p in range(pairs)]
    gate = jnp.concatenate(
        [
            jnp.sum(jnp.where(picks[p], gate_ref[0, p : p + 1, :], 0.0), 1, keepdims=True)
            for p in range(pairs)
        ],
        0,
    )
    act = hidden_ref[0]
    for part in range(2):
        out = jnp.dot(act, w_ref[0, part], preferred_element_type=F32)
        out = (out * gate).astype(BF16)
        core = core_ref[0] if part == 0 else 1 - core_ref[0]
        for i in range(4):
            at = pl.ds(pl.multiple_of((2 * i + core) * share, share), share)
            y_ref[0, :, at] = out[:, i * share : (i + 1) * share]
    act = act.astype(F32)
    inner = jnp.sum(act * raw, 1, keepdims=True)
    for p in range(pairs):
        gg_ref[0, p : p + 1, :] = jnp.sum(
            jnp.where(picks[p], inner[p * SLOTS : (p + 1) * SLOTS], 0.0), 0, keepdims=True
        )
    hs_ref[0] = (act * gate).astype(BF16)
    grad = raw * gate
    pre_ref[0, :, :hidden] = (grad * slope_ref[0].astype(F32)).astype(BF16)
    pre_ref[0, :, hidden:] = (grad * silu_ref[0].astype(F32)).astype(BF16)


def hidden_gradient(core, rows_cot, w_down_all, slots, gates, silu, slope, act):
    experts, rows, half = rows_cot[0].shape
    hidden = w_down_all.shape[2]
    _, pairs, tokens = slots.shape
    one = lambda *shape: pl.BlockSpec((1, *shape), lambda e, p: (e,) + (0,) * len(shape))
    wide = one(rows, hidden)
    return pl.pallas_call(
        hidden_kernel,
        grid_spec=pltpu.PrefetchScalarGridSpec(
            num_scalar_prefetch=1,
            grid=(experts,),
            in_specs=[
                one(rows, half),
                one(rows, half),
                one(2, hidden, half),
                one(pairs, tokens),
                one(pairs, tokens),
                wide,
                wide,
                wide,
            ],
            out_specs=[
                one(rows, 2 * hidden),
                wide,
                one(rows, 2 * half),
                one(pairs, tokens),
            ],
        ),
        out_shape=[
            jax.ShapeDtypeStruct((experts, rows, 2 * hidden), BF16),
            jax.ShapeDtypeStruct((experts, rows, hidden), BF16),
            jax.ShapeDtypeStruct((experts, rows, 2 * half), BF16),
            jax.ShapeDtypeStruct((experts, pairs, tokens), F32),
        ],
        compiler_params=params(),
        cost_estimate=cost(8 * rows * half * hidden * experts, 23 << 20),
    )(core, *rows_cot, w_down_all, slots, gates, silu, slope, act)


def shares_kernel(core_ref, w_own_ref, w_other_ref, own_ref, other_ref):
    own_ref[...] = w_own_ref[0]
    other_ref[...] = w_other_ref[0]


def column_shares(core, w, share):
    _, rows, width = w.shape
    out = jax.ShapeDtypeStruct((rows, width // 2), w.dtype)
    return pl.pallas_call(
        shares_kernel,
        grid_spec=pltpu.PrefetchScalarGridSpec(
            num_scalar_prefetch=1,
            grid=(width // (2 * share),),
            in_specs=[
                pl.BlockSpec((1, rows, share), lambda i, c: (0, 0, 2 * i + c[0])),
                pl.BlockSpec((1, rows, share), lambda i, c: (0, 0, 2 * i + 1 - c[0])),
            ],
            out_specs=[pl.BlockSpec((rows, share), lambda i, c: (0, i))] * 2,
        ),
        out_shape=[out, out],
        compiler_params=params(),
        cost_estimate=cost(0, 3 << 20),
    )(core, w, w)


def output_kernel(place_ref, slot_ref, y_ref, out_ref, pick_ref):
    pairs, experts, tokens = slot_ref.shape
    block = tokens // 2
    columns = out_ref.shape[2]

    @pl.when(pl.program_id(0) == 0)
    def _():
        for p in range(pairs):
            pick = jnp.concatenate(
                [chosen(slot_ref[p, e : e + 1, :]).astype(BF16) for e in range(experts)], 0
            )
            pick_ref[p] = pick.T

    for p in range(pairs):
        y = y_ref[:, p].reshape(experts * SLOTS, columns)
        total = jnp.dot(pick_ref[p], y, preferred_element_type=F32).astype(BF16)
        for j in range(2):
            out_ref[pl.ds(place_ref[2 * p + j], 1)] = total[j * block : (j + 1) * block].reshape(
                1, block, columns
            )


def output_rows(place, slots, y):
    pairs, experts, tokens = slots.shape
    width = y.shape[3]
    columns = 512
    return pl.pallas_call(
        output_kernel,
        grid_spec=pltpu.PrefetchScalarGridSpec(
            num_scalar_prefetch=1,
            grid=(width // columns,),
            in_specs=[
                pl.BlockSpec((pairs, experts, tokens), lambda n, p: (0, 0, 0)),
                pl.BlockSpec((experts, pairs, SLOTS, columns), lambda n, p: (0, 0, 0, n)),
            ],
            out_specs=pl.BlockSpec((2 * pairs, tokens // 2, columns), lambda n, p: (0, 0, n)),
            scratch_shapes=[pltpu.VMEM((pairs, tokens, experts * SLOTS), BF16)],
        ),
        out_shape=jax.ShapeDtypeStruct((2 * pairs, tokens // 2, width), BF16),
        compiler_params=params(),
        cost_estimate=cost(2 * pairs * experts * SLOTS * tokens * width, 10 << 20),
    )(place, slots, y)


def weight_kernel(place_ref, *refs):
    (x, c, pre, hs), (x2, c2, pre2, hs2) = refs[:4], refs[4:8]
    first_ref, second_ref = refs[8:]
    columns = pre.shape[2]
    hidden = hs.shape[2]
    ring, _, half, _ = second_ref.shape
    share = x.shape[2] // ring
    piece = hidden // 3
    hst, hst2 = hs[0].T, hs2[0].T
    for i in range(ring):
        at = slice(i * share, (i + 1) * share)
        grad_in = jnp.dot(x[0, :, at].T, pre[0], preferred_element_type=F32)
        grad_in += jnp.dot(x2[0, :, at].T, pre2[0], preferred_element_type=F32)
        down = jnp.dot(hst, c[0, :, at], preferred_element_type=F32)
        down += jnp.dot(hst2, c2[0, :, at], preferred_element_type=F32)
        to = pl.ds(place_ref[i], 1)
        first_ref[0, to] = grad_in[:half].astype(BF16).reshape(1, half, columns)
        packed = jnp.concatenate([down[n * piece : (n + 1) * piece] for n in range(3)], 1)
        second_ref[to, 0] = (
            jnp.concatenate([grad_in[half:], packed], 0).astype(BF16).reshape(1, half, columns)
        )


def weight_gradient(place, ours, theirs):
    x, _, pre, hs = ours
    experts, rows, columns = pre.shape
    hidden = hs.shape[2]
    ring = 4
    half = (x.shape[2] // ring + hidden // 3) // 2
    one = lambda *shape: pl.BlockSpec((1, *shape), lambda e, p: (e,) + (0,) * len(shape))
    specs = [one(*value.shape[1:]) for value in ours]
    return pl.pallas_call(
        weight_kernel,
        grid_spec=pltpu.PrefetchScalarGridSpec(
            num_scalar_prefetch=1,
            grid=(experts,),
            in_specs=specs * 2,
            out_specs=[
                pl.BlockSpec((1, ring, half, columns), lambda e, p: (e, 0, 0, 0)),
                pl.BlockSpec((ring, 1, half, columns), lambda e, p: (0, e, 0, 0)),
            ],
        ),
        out_shape=[
            jax.ShapeDtypeStruct((experts, ring, half, columns), BF16),
            jax.ShapeDtypeStruct((ring, experts, half, columns), BF16),
        ],
        compiler_params=params(),
        cost_estimate=cost(4 * rows * x.shape[2] * 3 * hidden * experts, 26 << 20),
    )(place, *ours, *theirs)


def shift(value, axis, by):
    n = lax.axis_size(axis)
    return lax.ppermute(value, axis, [(i, (i + by) % n) for i in range(n)])


def ring_blocks(block, rows, axis):
    n = lax.axis_size(axis)
    got = {0: [block]}
    below = above = block
    for step in range(1, n // 2):
        below, above = shift(below, axis, 1), shift(above, axis, -1)
        got[step], got[n - step] = [below], [above]
    got[n // 2] = [shift(below[:rows], axis, 1), shift(above[rows:], axis, -1)]
    return got


def in_three(value):
    parts = []
    for _ in range(3):
        parts.append(lax.reduce_precision(value, 8, 7))
        value = value - parts[-1]
    return parts


def add(*terms):
    total = terms[0].astype(F32)
    for term in terms[1:]:
        total = total + term.astype(F32)
    return total


def ring_scatter(parts, axis, kind):
    half = parts[0].shape[0] // 2
    low = shift(parts[2][:half], axis, 1)
    high = shift(parts[2][half:], axis, -1)
    to_up = jnp.concatenate([add(parts[1][:half], low).astype(BF16), parts[1][half:]], 0)
    to_down = jnp.concatenate([parts[3][:half], add(parts[3][half:], high).astype(BF16)], 0)
    low, high = shift(to_up, axis, 1), shift(to_down, axis, -1)
    return add(parts[0], low, high).astype(kind)


def swap_cores(value):
    return lax.ppermute(value, "core", [(0, 1), (1, 0)])


def on_device(tokens, gates, routes, cotangent, w_in, w_down):
    block, width = tokens.shape
    hidden = w_down.shape[1]
    top = routes.shape[1]
    x_at, core_at = lax.axis_index("x"), lax.axis_index("core")
    z_at, y_at = lax.axis_index("z"), lax.axis_index("y")
    z_size, y_size = lax.axis_size("z"), lax.axis_size("y")
    pairs = len(PAIRS)
    experts_at = jnp.remainder(y_at + jnp.arange(y_size), y_size).astype(jnp.int32)

    depth = width // 8
    share_in = lax.dynamic_slice_in_dim(w_in[0], (x_at * 2 + core_at) * depth, depth, 0)
    w_in_all = lax.all_gather(share_in, ("x", "core", "y"), axis=0, tiled=True)
    w_in_all = w_in_all.reshape(4, 2, y_size, depth, 2 * hidden)

    choices = jnp.concatenate([routes.T.astype(F32), *in_three(gates.T)], 0).astype(BF16)
    lines = choices.size // width
    extra = jnp.pad(choices.reshape(lines, width), ((0, LINES - lines), (0, 0)))
    ring_tokens = ring_blocks(jnp.concatenate([tokens, extra], 0), block // 2, "z")
    ring_cot = ring_blocks(cotangent, block // 2, "z")
    core = core_at.astype(jnp.int32)[None]
    meta = jnp.concatenate([core, z_at * y_size + experts_at]).astype(jnp.int32)

    def routed(ring, slots):
        buffers, found = [], []
        for p, pair in enumerate(PAIRS):
            pieces = [(piece, block // len(ring[d])) for d in pair for piece in ring[d]]
            given = slots[p] if slots else None
            out = select(p, meta, pieces, given, buffers)
            buffers = out[:2]
            found.append(out[2:])
        return [
            value.reshape(y_size, pairs * SLOTS, width // 2) for value in buffers
        ], found

    rows_in, found = routed(ring_tokens, None)
    rows_cot, _ = routed(ring_cot, [slot for slot, _ in found])
    slots = jnp.concatenate([slot for slot, _ in found], 0)
    expert_slots = jnp.swapaxes(slots, 0, 1)
    gate_of = jnp.swapaxes(jnp.concatenate([gate for _, gate in found], 0), 0, 1)

    own, rest = column_shares(core, w_down, depth)
    below, above = shift(own, "y", 1), shift(own, "y", -1)
    cut = hidden // 2
    far = jnp.concatenate([shift(below[:cut], "y", 1), shift(above[cut:], "y", -1)], 0)
    w_down_all = jnp.stack(
        [jnp.stack([own, rest])]
        + [jnp.stack([held, swap_cores(held)]) for held in (above, far, below)]
    )

    silu, slope, act = forward(jnp.concatenate([experts_at, core]), rows_in, w_in_all)
    pre, hs, y, gg = hidden_gradient(
        core, rows_cot, w_down_all, expert_slots, gate_of, silu, slope, act
    )
    ours = (rows_in[0], rows_cot[0], pre, hs)
    theirs = [swap_cores(value) for value in (rows_in[1], rows_cot[1], pre, hs)]
    place = jnp.remainder(z_at - jnp.array(DISTANCES), z_size).astype(jnp.int32)
    partial = output_rows(place, slots, y.reshape(y_size, pairs, SLOTS, width))
    mixed_out = lax.psum_scatter(partial, "z", scatter_dimension=0, tiled=True)[0]
    x_places = jnp.remainder(jnp.arange(4) - x_at, 4).astype(jnp.int32)
    first, second = weight_gradient(x_places, ours, theirs)
    first = ring_scatter([first[i] for i in range(4)], "y", BF16)
    second = ring_scatter([second[i] for i in range(4)], "x", BF16)
    first = ring_scatter([first[i] for i in range(4)], "x", F32)
    second = ring_scatter([second[i] for i in range(4)], "y", F32)

    left = depth - first.shape[0]
    grad_in = jnp.concatenate([first, second[:left]], 0)
    packed = second[left:]
    grad_down = jnp.concatenate([packed[:, i * depth : (i + 1) * depth] for i in range(3)], 0)

    lines_of = jnp.concatenate(
        [ring_tokens[d][-1][-LINES:][: top * block // width + 1] for d in DISTANCES], 0
    ).reshape(z_size, -1, block)[:, :top]
    hit = lines_of.astype(jnp.int32)[:, None] == (z_at * y_size + experts_at)[None, :, None, None]
    gg = gg.reshape(y_size, pairs, 2, block).transpose(1, 2, 0, 3).reshape(z_size, y_size, block)
    gg = jnp.sum(jnp.where(hit, gg[:, :, None], 0.0), 1)
    gg = jnp.stack([gg[DISTANCES.index(d)] for d in range(z_size)])
    for by in (4, 2, 1):
        gg = gg[:by] + shift(gg[by:], "z", -by)
    return mixed_out, gg[0].T, grad_in[None], grad_down[None]


def solution(mesh):
    wide = Mesh(mesh.devices.reshape(4, 2, 8, 4), ("x", "core", "z", "y"))
    rows = P(("x", "core", "z", "y"), None)
    expert = P(("z", "y"), None, None)
    return jax.shard_map(
        on_device,
        mesh=wide,
        in_specs=(rows, rows, rows, rows, expert, expert),
        out_specs=(
            rows,
            rows,
            P(("z", "y"), ("x", "core"), None),
            P(("z", "y"), None, ("x", "core")),
        ),
        check_vma=False,
    )
```

```python
import jax
import jax.numpy as jnp
from jax import lax
from jax.experimental import pallas as pl
from jax.experimental.pallas import tpu as pltpu
from jax.sharding import Mesh, PartitionSpec as P

BF16 = jnp.bfloat16
F32 = jnp.float32
VMEM_BYTES = 48 * 1024 * 1024
SLOTS = 80
PAIRS = ((1, 7), (2, 6), (3, 5), (0, 4))
DISTANCES = tuple(d for pair in PAIRS for d in pair)
SPAN = 128
TOP = 8
LINES = 16


def params(steps=1):
    return pltpu.CompilerParams(
        dimension_semantics=("arbitrary",) * steps, vmem_limit_bytes=VMEM_BYTES
    )


def cost(flops, moved):
    return pl.CostEstimate(flops=flops, bytes_accessed=moved, transcendentals=0)


def chosen(slot_row):
    tokens = slot_row.shape[1]
    return lax.broadcasted_iota(jnp.int32, (SLOTS, tokens), 0) == slot_row


def places(meta_ref, lines_refs):
    width = lines_refs[0].shape[1]
    block = SPAN
    at = lambda ref, i: ref[
        i * block // width : i * block // width + 1, i * block % width : i * block % width + block
    ].astype(F32)
    hits, gates = [], []
    for ref in lines_refs:
        routes = [at(ref, k) for k in range(TOP)]
        parts = [at(ref, TOP + k) for k in range(3 * TOP)]
        weights = [parts[k] + parts[TOP + k] + parts[2 * TOP + k] for k in range(TOP)]
        for e in range(4):
            mine = meta_ref[1 + e].astype(F32)
            hit = jnp.zeros((1, block), F32)
            gate = jnp.zeros((1, block), F32)
            for k in range(TOP):
                same = routes[k] == mine
                hit = jnp.where(same, 1.0, hit)
                gate = jnp.where(same, weights[k], gate)
            hits.append(hit)
            gates.append(gate)
    hit = jnp.concatenate(hits, 0)
    row = lax.broadcasted_iota(jnp.int32, (block, block), 0)
    column = lax.broadcasted_iota(jnp.int32, (block, block), 1)
    earlier = jnp.where(row < column, 1.0, 0.0).astype(BF16)
    rank = jnp.dot(hit.astype(BF16), earlier, preferred_element_type=F32)
    slot = jnp.where(hit > 0.5, rank, -float(SLOTS)).astype(jnp.int32)
    slot = jnp.concatenate(
        [slot[:4], jnp.where(slot[4:] < 0, slot[4:], slot[4:] + SLOTS // 2)], 1
    )
    return slot, jnp.concatenate(
        [jnp.concatenate(gates[:4], 0), jnp.concatenate(gates[4:], 0)], 1
    )


def select_kernel(count, lines, meta_ref, *refs):
    pieces, rows_ref = refs[:count], refs[-1]
    if lines:
        slot, gate = places(meta_ref, refs[count : count + 2])
        slot_ref, gate_ref = refs[-3], refs[-2]
        slot_ref[0] = slot
        gate_ref[0] = gate
        outs = refs[-5:-3]
    else:
        slot = refs[count][0]
        outs = refs[-3:-1]
    experts = slot.shape[0]
    at = 0
    for piece in pieces:
        rows_ref[at : at + piece.shape[0], :] = piece[...]
        at += piece.shape[0]
    pick = jnp.concatenate([chosen(slot[e : e + 1]).astype(BF16) for e in range(experts)], 0)
    share = outs[0].shape[3] // 4
    for part, out_ref in enumerate(outs):
        core = meta_ref[0] if part == 0 else 1 - meta_ref[0]
        for i in range(4):
            at = pl.ds(pl.multiple_of((2 * i + core) * share, share), share)
            got = jnp.dot(pick, rows_ref[:, at], preferred_element_type=F32).astype(BF16)
            out_ref[:, 0, :, i * share : (i + 1) * share] = got.reshape(experts, SLOTS, share)


def select(pair, meta, pieces, slots, buffers):
    experts, pairs, tokens = 4, len(PAIRS), 2 * SPAN
    width = pieces[0][0].shape[1]
    operands = [meta, *(array for array, _ in pieces)]
    in_specs = [pl.BlockSpec((rows, width), lambda i, c: (0, 0)) for _, rows in pieces]
    out_shape = [jax.ShapeDtypeStruct((experts, pairs, SLOTS, width // 2), BF16)] * 2
    out_specs = [
        pl.BlockSpec((experts, 1, SLOTS, width // 2), lambda i, c: (0, pair, 0, 0))
    ] * 2
    small = pl.BlockSpec((1, experts, tokens), lambda i, c: (0, 0, 0))
    if slots is None:
        for array, rows in pieces:
            if array.shape[0] > rows:
                operands.append(array)
                in_specs.append(
                    pl.BlockSpec((LINES, width), lambda i, c, at=rows // LINES: (at, 0))
                )
        out_shape += [
            jax.ShapeDtypeStruct((1, experts, tokens), kind) for kind in (jnp.int32, F32)
        ]
        out_specs += [small, small]
    else:
        operands.append(slots)
        in_specs.append(small)
    aliases = {}
    if buffers:
        aliases = {len(operands) + i: i for i in range(2)}
        operands += buffers
        in_specs += [pl.BlockSpec(memory_space=pl.ANY)] * 2
    count = len(pieces)
    return pl.pallas_call(
        lambda *refs: select_kernel(count, slots is None, *refs),
        grid_spec=pltpu.PrefetchScalarGridSpec(
            num_scalar_prefetch=1,
            grid=(1,),
            in_specs=in_specs,
            out_specs=out_specs,
            scratch_shapes=[pltpu.VMEM((tokens, width), BF16)],
        ),
        out_shape=out_shape,
        input_output_aliases=aliases,
        compiler_params=params(),
        cost_estimate=cost(2 * experts * SLOTS * tokens * width, 3 << 20),
    )(*operands)


def forward_kernel(place_ref, own_ref, other_ref, w_own_ref, w_other_ref, *refs):
    silu_ref, slope_ref, hidden_ref = refs
    half = own_ref.shape[2]
    hidden = hidden_ref.shape[2]
    pre = jnp.dot(
        own_ref[0], w_own_ref[...].reshape(half, 2 * hidden), preferred_element_type=F32
    )
    pre += jnp.dot(
        other_ref[0], w_other_ref[...].reshape(half, 2 * hidden), preferred_element_type=F32
    )
    gate_pre, up_pre = pre[:, :hidden], pre[:, hidden:]
    sig = jax.nn.sigmoid(gate_pre)
    silu = gate_pre * sig
    silu_ref[0] = silu.astype(BF16)
    slope_ref[0] = (up_pre * sig * (1.0 + gate_pre * (1.0 - sig))).astype(BF16)
    hidden_ref[0] = (silu * up_pre).astype(BF16)


def forward(place, rows_in, w_in_all):
    experts, rows, half = rows_in[0].shape
    x_size, _, _, depth, columns = w_in_all.shape
    hidden = columns // 2
    out = jax.ShapeDtypeStruct((experts, rows, hidden), BF16)
    spec = pl.BlockSpec((1, rows, hidden), lambda e, p: (e, 0, 0))
    row_spec = pl.BlockSpec((1, rows, half), lambda e, p: (e, 0, 0))
    weights = (x_size, 1, 1, depth, columns)
    return pl.pallas_call(
        forward_kernel,
        grid_spec=pltpu.PrefetchScalarGridSpec(
            num_scalar_prefetch=1,
            grid=(experts,),
            in_specs=[
                row_spec,
                row_spec,
                pl.BlockSpec(weights, lambda e, p: (0, p[4], p[e], 0, 0)),
                pl.BlockSpec(weights, lambda e, p: (0, 1 - p[4], p[e], 0, 0)),
            ],
            out_specs=[spec] * 3,
        ),
        out_shape=[out] * 3,
        compiler_params=params(),
        cost_estimate=cost(4 * rows * half * columns * experts, 21 << 20),
    )(place, *rows_in, w_in_all, w_in_all)


def hidden_kernel(
    core_ref, own_ref, other_ref, w_ref, slot_ref, gate_ref, silu_ref, slope_ref, hidden_ref,
    pre_ref, hs_ref, y_ref, gg_ref,
):
    hidden = hidden_ref.shape[2]
    share = own_ref.shape[2] // 4
    pairs = slot_ref.shape[1]
    across = (((1,), (1,)), ((), ()))
    raw = jnp.zeros((own_ref.shape[1], hidden), F32)
    for part, rows_ref in enumerate((own_ref, other_ref)):
        core = core_ref[0] if part == 0 else 1 - core_ref[0]
        for i in range(4):
            at = pl.ds(pl.multiple_of((2 * i + core) * share, share), share)
            raw += lax.dot_general(
                rows_ref[0, :, i * share : (i + 1) * share], w_ref[0, :, at], across,
                preferred_element_type=F32,
            )
    picks = [chosen(slot_ref[0, p : p + 1, :]) for p in range(pairs)]
    gate = jnp.concatenate(
        [
            jnp.sum(jnp.where(picks[p], gate_ref[0, p : p + 1, :], 0.0), 1, keepdims=True)
            for p in range(pairs)
        ],
        0,
    )
    act = hidden_ref[0]
    out = jnp.dot(act, w_ref[0], preferred_element_type=F32)
    y_ref[0] = (out * gate).astype(BF16)
    act = act.astype(F32)
    inner = jnp.sum(act * raw, 1, keepdims=True)
    for p in range(pairs):
        gg_ref[0, p : p + 1, :] = jnp.sum(
            jnp.where(picks[p], inner[p * SLOTS : (p + 1) * SLOTS], 0.0), 0, keepdims=True
        )
    hs_ref[0] = (act * gate).astype(BF16)
    grad = raw * gate
    pre_ref[0, :, :hidden] = (grad * slope_ref[0].astype(F32)).astype(BF16)
    pre_ref[0, :, hidden:] = (grad * silu_ref[0].astype(F32)).astype(BF16)


def hidden_gradient(core, rows_cot, w_down_all, slots, gates, silu, slope, act):
    experts, rows, half = rows_cot[0].shape
    hidden = w_down_all.shape[1]
    _, pairs, tokens = slots.shape
    one = lambda *shape: pl.BlockSpec((1, *shape), lambda e, p: (e,) + (0,) * len(shape))
    wide = one(rows, hidden)
    return pl.pallas_call(
        hidden_kernel,
        grid_spec=pltpu.PrefetchScalarGridSpec(
            num_scalar_prefetch=1,
            grid=(experts,),
            in_specs=[
                one(rows, half),
                one(rows, half),
                pl.BlockSpec((1, hidden, 2 * half), lambda e, p: (p[1 + e], 0, 0)),
                one(pairs, tokens),
                one(pairs, tokens),
                wide,
                wide,
                wide,
            ],
            out_specs=[
                one(rows, 2 * hidden),
                wide,
                one(rows, 2 * half),
                one(pairs, tokens),
            ],
        ),
        out_shape=[
            jax.ShapeDtypeStruct((experts, rows, 2 * hidden), BF16),
            jax.ShapeDtypeStruct((experts, rows, hidden), BF16),
            jax.ShapeDtypeStruct((experts, rows, 2 * half), BF16),
            jax.ShapeDtypeStruct((experts, pairs, tokens), F32),
        ],
        compiler_params=params(),
        cost_estimate=cost(8 * rows * half * hidden * experts, 23 << 20),
    )(core, *rows_cot, w_down_all, slots, gates, silu, slope, act)


def output_kernel(place_ref, slot_ref, y_ref, out_ref, pick_ref):
    pairs, experts, tokens = slot_ref.shape
    block = tokens // 2
    columns = out_ref.shape[2]

    @pl.when(pl.program_id(0) == 0)
    def _():
        for p in range(pairs):
            pick = jnp.concatenate(
                [chosen(slot_ref[p, e : e + 1, :]).astype(BF16) for e in range(experts)], 0
            )
            pick_ref[p] = pick.T

    for p in range(pairs):
        y = y_ref[:, p].reshape(experts * SLOTS, columns)
        total = jnp.dot(pick_ref[p], y, preferred_element_type=F32).astype(BF16)
        for j in range(2):
            out_ref[pl.ds(place_ref[2 * p + j], 1)] = total[j * block : (j + 1) * block].reshape(
                1, block, columns
            )


def output_rows(place, slots, y):
    pairs, experts, tokens = slots.shape
    width = y.shape[3]
    columns = 512
    return pl.pallas_call(
        output_kernel,
        grid_spec=pltpu.PrefetchScalarGridSpec(
            num_scalar_prefetch=1,
            grid=(width // columns,),
            in_specs=[
                pl.BlockSpec((pairs, experts, tokens), lambda n, p: (0, 0, 0)),
                pl.BlockSpec((experts, pairs, SLOTS, columns), lambda n, p: (0, 0, 0, n)),
            ],
            out_specs=pl.BlockSpec((2 * pairs, tokens // 2, columns), lambda n, p: (0, 0, n)),
            scratch_shapes=[pltpu.VMEM((pairs, tokens, experts * SLOTS), BF16)],
        ),
        out_shape=jax.ShapeDtypeStruct((2 * pairs, tokens // 2, width), BF16),
        compiler_params=pltpu.CompilerParams(vmem_limit_bytes=60 * 1024 * 1024),
        cost_estimate=cost(2 * pairs * experts * SLOTS * tokens * width, 10 << 20),
    )(place, slots, y)


def weight_kernel(place_ref, *refs):
    (x, c, pre, hs), (x2, c2, pre2, hs2) = refs[:4], refs[4:8]
    first_ref, second_ref = refs[8:]
    columns = pre.shape[2]
    hidden = hs.shape[2]
    ring, _, half, _ = second_ref.shape
    share = x.shape[2] // ring
    piece = hidden // 3
    hst, hst2 = hs[0].T, hs2[0].T
    for i in range(ring):
        at = slice(i * share, (i + 1) * share)
        grad_in = jnp.dot(x[0, :, at].T, pre[0], preferred_element_type=F32)
        grad_in += jnp.dot(x2[0, :, at].T, pre2[0], preferred_element_type=F32)
        down = jnp.dot(hst, c[0, :, at], preferred_element_type=F32)
        down += jnp.dot(hst2, c2[0, :, at], preferred_element_type=F32)
        to = pl.ds(place_ref[i], 1)
        first_ref[0, to] = grad_in[:half].astype(BF16).reshape(1, half, columns)
        packed = jnp.concatenate([down[n * piece : (n + 1) * piece] for n in range(3)], 1)
        second_ref[to, 0] = (
            jnp.concatenate([grad_in[half:], packed], 0).astype(BF16).reshape(1, half, columns)
        )


def weight_gradient(place, ours, theirs):
    x, _, pre, hs = ours
    experts, rows, columns = pre.shape
    hidden = hs.shape[2]
    ring = 4
    half = (x.shape[2] // ring + hidden // 3) // 2
    one = lambda *shape: pl.BlockSpec((1, *shape), lambda e, p: (e,) + (0,) * len(shape))
    specs = [one(*value.shape[1:]) for value in ours]
    return pl.pallas_call(
        weight_kernel,
        grid_spec=pltpu.PrefetchScalarGridSpec(
            num_scalar_prefetch=1,
            grid=(experts,),
            in_specs=specs * 2,
            out_specs=[
                pl.BlockSpec((1, ring, half, columns), lambda e, p: (e, 0, 0, 0)),
                pl.BlockSpec((ring, 1, half, columns), lambda e, p: (0, e, 0, 0)),
            ],
        ),
        out_shape=[
            jax.ShapeDtypeStruct((experts, ring, half, columns), BF16),
            jax.ShapeDtypeStruct((ring, experts, half, columns), BF16),
        ],
        compiler_params=params(),
        cost_estimate=cost(4 * rows * x.shape[2] * 3 * hidden * experts, 26 << 20),
    )(place, *ours, *theirs)


def shift(value, axis, by):
    n = lax.axis_size(axis)
    return lax.ppermute(value, axis, [(i, (i + by) % n) for i in range(n)])


def ring_blocks(block, rows, axis):
    n = lax.axis_size(axis)
    got = {0: [block]}
    below = above = block
    for step in range(1, n // 2):
        below, above = shift(below, axis, 1), shift(above, axis, -1)
        got[step], got[n - step] = [below], [above]
    got[n // 2] = [shift(below[:rows], axis, 1), shift(above[rows:], axis, -1)]
    return got


def in_three(value):
    parts = []
    for _ in range(3):
        parts.append(lax.reduce_precision(value, 8, 7))
        value = value - parts[-1]
    return parts


def add(*terms):
    total = terms[0].astype(F32)
    for term in terms[1:]:
        total = total + term.astype(F32)
    return total


def ring_scatter(parts, axis, kind):
    half = parts[0].shape[0] // 2
    low = shift(parts[2][:half], axis, 1)
    high = shift(parts[2][half:], axis, -1)
    to_up = jnp.concatenate([add(parts[1][:half], low).astype(BF16), parts[1][half:]], 0)
    to_down = jnp.concatenate([parts[3][:half], add(parts[3][half:], high).astype(BF16)], 0)
    low, high = shift(to_up, axis, 1), shift(to_down, axis, -1)
    return add(parts[0], low, high).astype(kind)


def swap_cores(value):
    return lax.ppermute(value, "core", [(0, 1), (1, 0)])


def on_device(tokens, gates, routes, cotangent, w_in, w_down):
    block, width = tokens.shape
    hidden = w_down.shape[1]
    top = routes.shape[1]
    x_at, core_at = lax.axis_index("x"), lax.axis_index("core")
    z_at, y_at = lax.axis_index("z"), lax.axis_index("y")
    z_size, y_size = lax.axis_size("z"), lax.axis_size("y")
    pairs = len(PAIRS)
    experts_at = jnp.remainder(y_at + jnp.arange(y_size), y_size).astype(jnp.int32)

    depth = width // 8
    share_in = lax.dynamic_slice_in_dim(w_in[0], (x_at * 2 + core_at) * depth, depth, 0)
    w_in_all = lax.all_gather(share_in, ("x", "core", "y"), axis=0, tiled=True)
    w_in_all = w_in_all.reshape(4, 2, y_size, depth, 2 * hidden)

    choices = jnp.concatenate([routes.T.astype(F32), *in_three(gates.T)], 0).astype(BF16)
    lines = choices.size // width
    extra = jnp.pad(choices.reshape(lines, width), ((0, LINES - lines), (0, 0)))
    ring_tokens = ring_blocks(jnp.concatenate([tokens, extra], 0), block // 2, "z")
    ring_cot = ring_blocks(cotangent, block // 2, "z")
    core = core_at.astype(jnp.int32)[None]
    meta = jnp.concatenate([core, z_at * y_size + experts_at]).astype(jnp.int32)

    def routed(ring, slots):
        buffers, found = [], []
        for p, pair in enumerate(PAIRS):
            pieces = [(piece, block // len(ring[d])) for d in pair for piece in ring[d]]
            given = slots[p] if slots else None
            out = select(p, meta, pieces, given, buffers)
            buffers = out[:2]
            found.append(out[2:])
        return [
            value.reshape(y_size, pairs * SLOTS, width // 2) for value in buffers
        ], found

    rows_in, found = routed(ring_tokens, None)
    rows_cot, _ = routed(ring_cot, [slot for slot, _ in found])
    slots = jnp.concatenate([slot for slot, _ in found], 0)
    expert_slots = jnp.swapaxes(slots, 0, 1)
    gate_of = jnp.swapaxes(jnp.concatenate([gate for _, gate in found], 0), 0, 1)

    def toward(value):
        pairs = [
            ((0, i), (0, (i - 1) % y_size)) for i in range(y_size)
        ] + [((1, i), (1, (i + 1) % y_size)) for i in range(y_size)]
        flat = [(a * y_size + i, b * y_size + j) for (a, i), (b, j) in pairs]
        return lax.ppermute(value, ("core", "y"), flat)

    cut = hidden // 2
    near = toward(w_down[0])
    far = toward(lax.dynamic_slice_in_dim(near, core_at * cut, cut, 0))
    near_other, far_other = swap_cores(near), swap_cores(far)
    far = jnp.where(
        core_at == 0, jnp.concatenate([far, far_other], 0), jnp.concatenate([far_other, far], 0)
    )
    w_down_all = jnp.stack([w_down[0], near, far, near_other])
    stacked = jnp.where(core_at == 0, jnp.arange(4), jnp.remainder(-jnp.arange(4), 4))
    stacked = jnp.concatenate([core, stacked.astype(jnp.int32)])

    silu, slope, act = forward(jnp.concatenate([experts_at, core]), rows_in, w_in_all)
    pre, hs, y, gg = hidden_gradient(
        stacked, rows_cot, w_down_all, expert_slots, gate_of, silu, slope, act
    )
    ours = (rows_in[0], rows_cot[0], pre, hs)
    theirs = [swap_cores(value) for value in (rows_in[1], rows_cot[1], pre, hs)]
    place = jnp.remainder(z_at - jnp.array(DISTANCES), z_size).astype(jnp.int32)
    partial = output_rows(place, slots, y.reshape(y_size, pairs, SLOTS, width))
    mixed_out = lax.psum_scatter(partial, "z", scatter_dimension=0, tiled=True)[0]
    x_places = jnp.remainder(jnp.arange(4) - x_at, 4).astype(jnp.int32)
    first, second = weight_gradient(x_places, ours, theirs)
    first = ring_scatter([first[i] for i in range(4)], "y", BF16)
    second = ring_scatter([second[i] for i in range(4)], "x", BF16)
    first = ring_scatter([first[i] for i in range(4)], "x", F32)
    second = ring_scatter([second[i] for i in range(4)], "y", F32)

    left = depth - first.shape[0]
    grad_in = jnp.concatenate([first, second[:left]], 0)
    packed = second[left:]
    grad_down = jnp.concatenate([packed[:, i * depth : (i + 1) * depth] for i in range(3)], 0)

    gg = gg.reshape(y_size, pairs, 2, block).transpose(1, 2, 0, 3).reshape(z_size, y_size, block)
    gg = {d: gg[i] for i, d in enumerate(DISTANCES)}
    for by in (1, 2, 4):
        moved = [d for d in range(z_size) if d & by]
        got = shift(jnp.stack([gg[d] for d in moved]), "z", -by)
        gg.update({d: got[i] for i, d in enumerate(moved)})
    gg = jnp.stack([gg[d] for d in range(z_size)])
    named = jnp.remainder(z_at + jnp.arange(z_size), z_size)[:, None] * y_size + experts_at
    same = routes.T[None, None] == named[:, :, None, None]
    grad_gates = jnp.sum(jnp.where(same, gg[:, :, None], 0.0), (0, 1)).T
    return mixed_out, grad_gates, grad_in[None], grad_down[None]


def solution(mesh):
    wide = Mesh(mesh.devices.reshape(4, 2, 8, 4), ("x", "core", "z", "y"))
    rows = P(("x", "core", "z", "y"), None)
    expert = P(("z", "y"), None, None)
    return jax.shard_map(
        on_device,
        mesh=wide,
        in_specs=(rows, rows, rows, rows, expert, expert),
        out_specs=(
            rows,
            rows,
            P(("z", "y"), ("x", "core"), None),
            P(("z", "y"), None, ("x", "core")),
        ),
        check_vma=False,
    )
```

```python
import jax
import jax.numpy as jnp
from jax import lax
from jax.experimental import pallas as pl
from jax.experimental.pallas import tpu as pltpu
from jax.sharding import Mesh, PartitionSpec as P

BF16 = jnp.bfloat16
F32 = jnp.float32
VMEM_BYTES = 48 * 1024 * 1024
SLOTS = 80
PAIRS = ((1, 7), (2, 6), (3, 5), (0, 4))
DISTANCES = tuple(d for pair in PAIRS for d in pair)
SPAN = 128
TOP = 8
LINES = 16


def params(steps=1):
    return pltpu.CompilerParams(
        dimension_semantics=("arbitrary",) * steps, vmem_limit_bytes=VMEM_BYTES
    )


def cost(flops, moved):
    return pl.CostEstimate(flops=flops, bytes_accessed=moved, transcendentals=0)


def chosen(slot_row):
    tokens = slot_row.shape[1]
    return lax.broadcasted_iota(jnp.int32, (SLOTS, tokens), 0) == slot_row


def places(meta_ref, lines_refs):
    width = lines_refs[0].shape[1]
    block = SPAN
    at = lambda ref, i: ref[
        i * block // width : i * block // width + 1, i * block % width : i * block % width + block
    ].astype(F32)
    hits, gates = [], []
    for ref in lines_refs:
        routes = [at(ref, k) for k in range(TOP)]
        parts = [at(ref, TOP + k) for k in range(3 * TOP)]
        weights = [parts[k] + parts[TOP + k] + parts[2 * TOP + k] for k in range(TOP)]
        for e in range(4):
            mine = meta_ref[1 + e].astype(F32)
            hit = jnp.zeros((1, block), F32)
            gate = jnp.zeros((1, block), F32)
            for k in range(TOP):
                same = routes[k] == mine
                hit = jnp.where(same, 1.0, hit)
                gate = jnp.where(same, weights[k], gate)
            hits.append(hit)
            gates.append(gate)
    hit = jnp.concatenate(hits, 0)
    row = lax.broadcasted_iota(jnp.int32, (block, block), 0)
    column = lax.broadcasted_iota(jnp.int32, (block, block), 1)
    earlier = jnp.where(row < column, 1.0, 0.0).astype(BF16)
    rank = jnp.dot(hit.astype(BF16), earlier, preferred_element_type=F32)
    slot = jnp.where(hit > 0.5, rank, -float(SLOTS)).astype(jnp.int32)
    slot = jnp.concatenate(
        [slot[:4], jnp.where(slot[4:] < 0, slot[4:], slot[4:] + SLOTS // 2)], 1
    )
    return slot, jnp.concatenate(
        [jnp.concatenate(gates[:4], 0), jnp.concatenate(gates[4:], 0)], 1
    )


def select_kernel(count, lines, through, meta_ref, *refs):
    pieces, rows_ref = refs[:count], refs[-1]
    if through:
        refs = (*refs[:-2], rows_ref)
    if lines:
        slot, gate = places(meta_ref, refs[count : count + 2])
        slot_ref, gate_ref = refs[-3], refs[-2]
        slot_ref[0] = slot
        gate_ref[0] = gate
        outs = refs[-5:-3]
    else:
        slot = refs[count][0]
        outs = refs[-3:-1]
    experts = slot.shape[0]
    at = 0
    for piece in pieces:
        rows_ref[at : at + piece.shape[0], :] = piece[...]
        at += piece.shape[0]
    pick = jnp.concatenate([chosen(slot[e : e + 1]).astype(BF16) for e in range(experts)], 0)
    share = outs[0].shape[3] // 4
    for part, out_ref in enumerate(outs):
        core = meta_ref[0] if part == 0 else 1 - meta_ref[0]
        for i in range(4):
            at = pl.ds(pl.multiple_of((2 * i + core) * share, share), share)
            got = jnp.dot(pick, rows_ref[:, at], preferred_element_type=F32).astype(BF16)
            out_ref[:, 0, :, i * share : (i + 1) * share] = got.reshape(experts, SLOTS, share)


def select(pair, meta, pieces, slots, buffers, after, through=None):
    experts, pairs, tokens = 4, len(PAIRS), 2 * SPAN
    width = pieces[0][0].shape[1]
    operands = [meta, *(array for array, _ in pieces)]
    in_specs = [pl.BlockSpec((rows, width), lambda i, c: (0, 0)) for _, rows in pieces]
    out_shape = [jax.ShapeDtypeStruct((experts, pairs, SLOTS, width // 2), BF16)] * 2
    out_specs = [
        pl.BlockSpec((experts, 1, SLOTS, width // 2), lambda i, c: (0, pair, 0, 0))
    ] * 2
    small = pl.BlockSpec((1, experts, tokens), lambda i, c: (0, 0, 0))
    if slots is None:
        for array, rows in pieces:
            if array.shape[0] > rows:
                operands.append(array)
                in_specs.append(
                    pl.BlockSpec((LINES, width), lambda i, c, at=rows // LINES: (at, 0))
                )
        out_shape += [
            jax.ShapeDtypeStruct((1, experts, tokens), kind) for kind in (jnp.int32, F32)
        ]
        out_specs += [small, small]
    else:
        operands.append(slots)
        in_specs.append(small)
    aliases = {}
    if buffers:
        aliases = {len(operands) + i: i for i in range(2)}
        operands += buffers
        in_specs += [pl.BlockSpec(memory_space=pl.ANY)] * 2
    if through is not None:
        aliases[len(operands)] = len(out_shape)
        operands.append(through)
        in_specs.append(pl.BlockSpec(memory_space=pl.ANY))
        out_shape.append(jax.ShapeDtypeStruct(through.shape, through.dtype))
        out_specs.append(pl.BlockSpec(memory_space=pl.ANY))
    operands += after
    in_specs += [pl.BlockSpec(memory_space=pl.ANY)] * len(after)
    count = len(pieces)
    return pl.pallas_call(
        lambda *refs: select_kernel(count, slots is None, through is not None, *refs),
        grid_spec=pltpu.PrefetchScalarGridSpec(
            num_scalar_prefetch=1,
            grid=(1,),
            in_specs=in_specs,
            out_specs=out_specs,
            scratch_shapes=[pltpu.VMEM((tokens, width), BF16)],
        ),
        out_shape=out_shape,
        input_output_aliases=aliases,
        compiler_params=params(),
        cost_estimate=cost(2 * experts * SLOTS * tokens * width, 3 << 20),
    )(*operands)


def forward_kernel(place_ref, own_ref, other_ref, w_own_ref, w_other_ref, *refs):
    silu_ref, slope_ref, hidden_ref = refs
    half = own_ref.shape[2]
    hidden = hidden_ref.shape[2]
    pre = jnp.dot(
        own_ref[0], w_own_ref[...].reshape(half, 2 * hidden), preferred_element_type=F32
    )
    pre += jnp.dot(
        other_ref[0], w_other_ref[...].reshape(half, 2 * hidden), preferred_element_type=F32
    )
    gate_pre, up_pre = pre[:, :hidden], pre[:, hidden:]
    sig = jax.nn.sigmoid(gate_pre)
    silu = gate_pre * sig
    silu_ref[0] = silu.astype(BF16)
    slope_ref[0] = (up_pre * sig * (1.0 + gate_pre * (1.0 - sig))).astype(BF16)
    hidden_ref[0] = (silu * up_pre).astype(BF16)


def forward(place, rows_in, w_in_all):
    experts, rows, half = rows_in[0].shape
    x_size, _, _, depth, columns = w_in_all.shape
    hidden = columns // 2
    out = jax.ShapeDtypeStruct((experts, rows, hidden), BF16)
    spec = pl.BlockSpec((1, rows, hidden), lambda e, p: (e, 0, 0))
    row_spec = pl.BlockSpec((1, rows, half), lambda e, p: (e, 0, 0))
    weights = (x_size, 1, 1, depth, columns)
    return pl.pallas_call(
        forward_kernel,
        grid_spec=pltpu.PrefetchScalarGridSpec(
            num_scalar_prefetch=1,
            grid=(experts,),
            in_specs=[
                row_spec,
                row_spec,
                pl.BlockSpec(weights, lambda e, p: (0, p[4], p[e], 0, 0)),
                pl.BlockSpec(weights, lambda e, p: (0, 1 - p[4], p[e], 0, 0)),
            ],
            out_specs=[spec] * 3,
        ),
        out_shape=[out] * 3,
        compiler_params=params(),
        cost_estimate=cost(4 * rows * half * columns * experts, 21 << 20),
    )(place, *rows_in, w_in_all, w_in_all)


def hidden_kernel(
    core_ref, own_ref, other_ref, w_ref, slot_ref, gate_ref, silu_ref, slope_ref, hidden_ref,
    pre_ref, hs_ref, y_ref, gg_ref,
):
    hidden = hidden_ref.shape[2]
    share = own_ref.shape[2] // 4
    pairs = slot_ref.shape[1]
    across = (((1,), (1,)), ((), ()))
    raw = jnp.zeros((own_ref.shape[1], hidden), F32)
    for part, rows_ref in enumerate((own_ref, other_ref)):
        core = core_ref[0] if part == 0 else 1 - core_ref[0]
        for i in range(4):
            at = pl.ds(pl.multiple_of((2 * i + core) * share, share), share)
            raw += lax.dot_general(
                rows_ref[0, :, i * share : (i + 1) * share], w_ref[0, :, at], across,
                preferred_element_type=F32,
            )
    picks = [chosen(slot_ref[0, p : p + 1, :]) for p in range(pairs)]
    gate = jnp.concatenate(
        [
            jnp.sum(jnp.where(picks[p], gate_ref[0, p : p + 1, :], 0.0), 1, keepdims=True)
            for p in range(pairs)
        ],
        0,
    )
    act = hidden_ref[0]
    out = jnp.dot(act, w_ref[0], preferred_element_type=F32)
    y_ref[0] = (out * gate).astype(BF16)
    act = act.astype(F32)
    inner = jnp.sum(act * raw, 1, keepdims=True)
    for p in range(pairs):
        gg_ref[0, p : p + 1, :] = jnp.sum(
            jnp.where(picks[p], inner[p * SLOTS : (p + 1) * SLOTS], 0.0), 0, keepdims=True
        )
    hs_ref[0] = (act * gate).astype(BF16)
    grad = raw * gate
    pre_ref[0, :, :hidden] = (grad * slope_ref[0].astype(F32)).astype(BF16)
    pre_ref[0, :, hidden:] = (grad * silu_ref[0].astype(F32)).astype(BF16)


def hidden_gradient(core, rows_cot, w_down_all, slots, gates, silu, slope, act):
    experts, rows, half = rows_cot[0].shape
    hidden = w_down_all.shape[1]
    _, pairs, tokens = slots.shape
    one = lambda *shape: pl.BlockSpec((1, *shape), lambda e, p: (e,) + (0,) * len(shape))
    wide = one(rows, hidden)
    return pl.pallas_call(
        hidden_kernel,
        grid_spec=pltpu.PrefetchScalarGridSpec(
            num_scalar_prefetch=1,
            grid=(experts,),
            in_specs=[
                one(rows, half),
                one(rows, half),
                pl.BlockSpec((1, hidden, 2 * half), lambda e, p: (p[1 + e], 0, 0)),
                one(pairs, tokens),
                one(pairs, tokens),
                wide,
                wide,
                wide,
            ],
            out_specs=[
                one(rows, 2 * hidden),
                wide,
                one(rows, 2 * half),
                one(pairs, tokens),
            ],
        ),
        out_shape=[
            jax.ShapeDtypeStruct((experts, rows, 2 * hidden), BF16),
            jax.ShapeDtypeStruct((experts, rows, hidden), BF16),
            jax.ShapeDtypeStruct((experts, rows, 2 * half), BF16),
            jax.ShapeDtypeStruct((experts, pairs, tokens), F32),
        ],
        compiler_params=params(),
        cost_estimate=cost(8 * rows * half * hidden * experts, 23 << 20),
    )(core, *rows_cot, w_down_all, slots, gates, silu, slope, act)


def output_kernel(place_ref, slot_ref, y_ref, out_ref, pick_ref):
    pairs, experts, tokens = slot_ref.shape
    block = tokens // 2
    columns = out_ref.shape[2]

    @pl.when(pl.program_id(0) == 0)
    def _():
        for p in range(pairs):
            pick = jnp.concatenate(
                [chosen(slot_ref[p, e : e + 1, :]).astype(BF16) for e in range(experts)], 0
            )
            pick_ref[p] = pick.T

    for p in range(pairs):
        y = y_ref[:, p].reshape(experts * SLOTS, columns)
        total = jnp.dot(pick_ref[p], y, preferred_element_type=F32).astype(BF16)
        for j in range(2):
            out_ref[pl.ds(place_ref[2 * p + j], 1)] = total[j * block : (j + 1) * block].reshape(
                1, block, columns
            )


def output_rows(place, slots, y):
    pairs, experts, tokens = slots.shape
    width = y.shape[3]
    columns = 512
    return pl.pallas_call(
        output_kernel,
        grid_spec=pltpu.PrefetchScalarGridSpec(
            num_scalar_prefetch=1,
            grid=(width // columns,),
            in_specs=[
                pl.BlockSpec((pairs, experts, tokens), lambda n, p: (0, 0, 0)),
                pl.BlockSpec((experts, pairs, SLOTS, columns), lambda n, p: (0, 0, 0, n)),
            ],
            out_specs=pl.BlockSpec((2 * pairs, tokens // 2, columns), lambda n, p: (0, 0, n)),
            scratch_shapes=[pltpu.VMEM((pairs, tokens, experts * SLOTS), BF16)],
        ),
        out_shape=jax.ShapeDtypeStruct((2 * pairs, tokens // 2, width), BF16),
        compiler_params=pltpu.CompilerParams(vmem_limit_bytes=60 * 1024 * 1024),
        cost_estimate=cost(2 * pairs * experts * SLOTS * tokens * width, 10 << 20),
    )(place, slots, y)


def weight_kernel(place_ref, *refs):
    (x, c, pre, hs), (x2, c2, pre2, hs2) = refs[:4], refs[4:8]
    first_ref, second_ref = refs[8:]
    columns = pre.shape[2]
    hidden = hs.shape[2]
    ring, _, half, _ = second_ref.shape
    share = x.shape[2] // ring
    piece = hidden // 3
    hst, hst2 = hs[0].T, hs2[0].T
    for i in range(ring):
        at = slice(i * share, (i + 1) * share)
        grad_in = jnp.dot(x[0, :, at].T, pre[0], preferred_element_type=F32)
        grad_in += jnp.dot(x2[0, :, at].T, pre2[0], preferred_element_type=F32)
        down = jnp.dot(hst, c[0, :, at], preferred_element_type=F32)
        down += jnp.dot(hst2, c2[0, :, at], preferred_element_type=F32)
        to = pl.ds(place_ref[i], 1)
        first_ref[0, to] = grad_in[:half].astype(BF16).reshape(1, half, columns)
        packed = jnp.concatenate([down[n * piece : (n + 1) * piece] for n in range(3)], 1)
        second_ref[to, 0] = (
            jnp.concatenate([grad_in[half:], packed], 0).astype(BF16).reshape(1, half, columns)
        )


def weight_gradient(place, ours, theirs):
    x, _, pre, hs = ours
    experts, rows, columns = pre.shape
    hidden = hs.shape[2]
    ring = 4
    half = (x.shape[2] // ring + hidden // 3) // 2
    one = lambda *shape: pl.BlockSpec((1, *shape), lambda e, p: (e,) + (0,) * len(shape))
    specs = [one(*value.shape[1:]) for value in ours]
    return pl.pallas_call(
        weight_kernel,
        grid_spec=pltpu.PrefetchScalarGridSpec(
            num_scalar_prefetch=1,
            grid=(experts,),
            in_specs=specs * 2,
            out_specs=[
                pl.BlockSpec((1, ring, half, columns), lambda e, p: (e, 0, 0, 0)),
                pl.BlockSpec((ring, 1, half, columns), lambda e, p: (0, e, 0, 0)),
            ],
        ),
        out_shape=[
            jax.ShapeDtypeStruct((experts, ring, half, columns), BF16),
            jax.ShapeDtypeStruct((ring, experts, half, columns), BF16),
        ],
        compiler_params=params(),
        cost_estimate=cost(4 * rows * x.shape[2] * 3 * hidden * experts, 26 << 20),
    )(place, *ours, *theirs)


def shift(value, axis, by):
    n = lax.axis_size(axis)
    return lax.ppermute(value, axis, [(i, (i + by) % n) for i in range(n)])


def in_three(value):
    parts = []
    for _ in range(3):
        parts.append(lax.reduce_precision(value, 8, 7))
        value = value - parts[-1]
    return parts


def add(*terms):
    total = terms[0].astype(F32)
    for term in terms[1:]:
        total = total + term.astype(F32)
    return total


def ring_scatter(parts, axis, kind):
    half = parts[0].shape[0] // 2
    low = shift(parts[2][:half], axis, 1)
    high = shift(parts[2][half:], axis, -1)
    to_up = jnp.concatenate([add(parts[1][:half], low).astype(BF16), parts[1][half:]], 0)
    to_down = jnp.concatenate([parts[3][:half], add(parts[3][half:], high).astype(BF16)], 0)
    low, high = shift(to_up, axis, 1), shift(to_down, axis, -1)
    return add(parts[0], low, high).astype(kind)


def swap_cores(value):
    return lax.ppermute(value, "core", [(0, 1), (1, 0)])


def on_device(tokens, gates, routes, cotangent, w_in, w_down):
    block, width = tokens.shape
    hidden = w_down.shape[1]
    top = routes.shape[1]
    x_at, core_at = lax.axis_index("x"), lax.axis_index("core")
    z_at, y_at = lax.axis_index("z"), lax.axis_index("y")
    z_size, y_size = lax.axis_size("z"), lax.axis_size("y")
    pairs = len(PAIRS)
    experts_at = jnp.remainder(y_at + jnp.arange(y_size), y_size).astype(jnp.int32)

    depth = width // 8
    share_in = lax.dynamic_slice_in_dim(w_in[0], (x_at * 2 + core_at) * depth, depth, 0)
    w_in_all = lax.all_gather(share_in, ("x", "core", "y"), axis=0, tiled=True)
    w_in_all = w_in_all.reshape(4, 2, y_size, depth, 2 * hidden)

    choices = jnp.concatenate([routes.T.astype(F32), *in_three(gates.T)], 0).astype(BF16)
    lines = choices.size // width
    extra = jnp.pad(choices.reshape(lines, width), ((0, LINES - lines), (0, 0)))
    core = core_at.astype(jnp.int32)[None]
    meta = jnp.concatenate([core, z_at * y_size + experts_at]).astype(jnp.int32)

    def toward(value):
        pairs = [
            ((0, i), (0, (i - 1) % y_size)) for i in range(y_size)
        ] + [((1, i), (1, (i + 1) % y_size)) for i in range(y_size)]
        flat = [(a * y_size + i, b * y_size + j) for (a, i), (b, j) in pairs]
        return lax.ppermute(value, ("core", "y"), flat)

    cut = hidden // 2
    near = toward(w_down[0])
    far = toward(lax.dynamic_slice_in_dim(near, core_at * cut, cut, 0))
    near_other, far_other = swap_cores(near), swap_cores(far)
    far = jnp.where(
        core_at == 0, jnp.concatenate([far, far_other], 0), jnp.concatenate([far_other, far], 0)
    )
    w_down_all = jnp.stack([w_down[0], near, far, near_other])
    stacked = jnp.where(core_at == 0, jnp.arange(4), jnp.remainder(-jnp.arange(4), 4))
    stacked = jnp.concatenate([core, stacked.astype(jnp.int32)])

    held = jnp.concatenate([tokens, extra], 0)
    ring_tokens, ring_cot = {0: [held]}, {0: [cotangent]}
    found, rows_in, rows_cot = [], [], []

    def pieces(ring, pair):
        return [(piece, block // len(ring[d])) for d in pair for piece in ring[d]]

    def pick_tokens(p, after, through):
        nonlocal rows_in
        out = select(p, meta, pieces(ring_tokens, PAIRS[p]), None, rows_in, after, through)
        rows_in = out[:2]
        found.append(out[2:4])
        return out[4:]

    def pick_cot(p, through):
        nonlocal rows_cot
        out = select(p, meta, pieces(ring_cot, PAIRS[p]), found[p][0], rows_cot, [], through)
        rows_cot = out[:2]
        return out[2:]

    for step in (1, 2, 3):
        for ring in (ring_tokens, ring_cot):
            ring[step] = [shift(ring[step - 1][0], "z", 1)]
            ring[z_size - step] = [shift(ring[(z_size - step + 1) % z_size][0], "z", -1)]
        if step > 1:
            ring_tokens[step] = pick_cot(step - 2, ring_tokens[step][0])
        ring_cot[step] = pick_tokens(step - 1, [], ring_cot[step][0])
    for ring in (ring_tokens, ring_cot):
        ring[4] = [
            shift(ring[3][0][: block // 2], "z", 1), shift(ring[5][0][block // 2 :], "z", -1)
        ]
    pick_cot(2, None)
    pick_tokens(3, [w_down_all], None)
    pick_cot(3, None)
    rows_in, rows_cot = [
        [value.reshape(y_size, pairs * SLOTS, width // 2) for value in rows]
        for rows in (rows_in, rows_cot)
    ]
    slots = jnp.concatenate([slot for slot, _ in found], 0)
    expert_slots = jnp.swapaxes(slots, 0, 1)
    gate_of = jnp.swapaxes(jnp.concatenate([gate for _, gate in found], 0), 0, 1)

    silu, slope, act = forward(jnp.concatenate([experts_at, core]), rows_in, w_in_all)
    pre, hs, y, gg = hidden_gradient(
        stacked, rows_cot, w_down_all, expert_slots, gate_of, silu, slope, act
    )
    ours = (rows_in[0], rows_cot[0], pre, hs)
    theirs = [swap_cores(value) for value in (rows_in[1], rows_cot[1], pre, hs)]
    place = jnp.remainder(z_at - jnp.array(DISTANCES), z_size).astype(jnp.int32)
    partial = output_rows(place, slots, y.reshape(y_size, pairs, SLOTS, width))
    mixed_out = lax.psum_scatter(partial, "z", scatter_dimension=0, tiled=True)[0]
    x_places = jnp.remainder(jnp.arange(4) - x_at, 4).astype(jnp.int32)
    first, second = weight_gradient(x_places, ours, theirs)
    first = ring_scatter([first[i] for i in range(4)], "y", BF16)
    second = ring_scatter([second[i] for i in range(4)], "x", BF16)
    first = ring_scatter([first[i] for i in range(4)], "x", F32)
    second = ring_scatter([second[i] for i in range(4)], "y", F32)

    left = depth - first.shape[0]
    grad_in = jnp.concatenate([first, second[:left]], 0)
    packed = second[left:]
    grad_down = jnp.concatenate([packed[:, i * depth : (i + 1) * depth] for i in range(3)], 0)

    gg = gg.reshape(y_size, pairs, 2, block).transpose(1, 2, 0, 3).reshape(z_size, y_size, block)
    gg = {d: gg[i] for i, d in enumerate(DISTANCES)}
    for by in (1, 2, 4):
        moved = [d for d in range(z_size) if d & by]
        got = shift(jnp.stack([gg[d] for d in moved]), "z", -by)
        gg.update({d: got[i] for i, d in enumerate(moved)})
    gg = jnp.stack([gg[d] for d in range(z_size)])
    named = jnp.remainder(z_at + jnp.arange(z_size), z_size)[:, None] * y_size + experts_at
    same = routes.T[None, None] == named[:, :, None, None]
    grad_gates = jnp.sum(jnp.where(same, gg[:, :, None], 0.0), (0, 1)).T
    return mixed_out, grad_gates, grad_in[None], grad_down[None]


def solution(mesh):
    wide = Mesh(mesh.devices.reshape(4, 2, 8, 4), ("x", "core", "z", "y"))
    rows = P(("x", "core", "z", "y"), None)
    expert = P(("z", "y"), None, None)
    return jax.shard_map(
        on_device,
        mesh=wide,
        in_specs=(rows, rows, rows, rows, expert, expert),
        out_specs=(
            rows,
            rows,
            P(("z", "y"), ("x", "core"), None),
            P(("z", "y"), None, ("x", "core")),
        ),
        check_vma=False,
    )
```
